256 devices in a mesh: band: 4 (over y_lo, core), pw: 64 (over z, y_hi, x).
Axes of the slice: x: 4, y: 4 (y_hi: 2, y_lo: 2; y = y_hi * 2 + y_lo), z: 8, core: 2. Of those that a mesh axis runs over, the one named last changes fastest.
Arguments:
- orbitals: bfloat16 [4, 2, 192, 16384], P('band', None, None, 'pw'), may hold values from -6 to 6
- column_map: int32 [16384], replicated, may hold values from 0 to 36863, as said below
- potential: float32 [192, 192, 192], P('pw'), may hold values from -1.5 to 1
- projectors: bfloat16 [32768, 8, 128], P('pw'), may hold values from -0.59765625 to 0.59765625
- block_index: int32 [32768], P('pw'), may hold values from 0 to 863, as said below
- block_atom: int32 [32768], P('pw'), may hold values from 0 to 1999, as said below
- coupling: float32 [2000, 8, 8], replicated, may hold values from -1.2 to 1.2
Outputs:
- applied: float32 [4, 2, 192, 16384], P('band', None, None, 'pw')
- subspace: float32 [2, 4, 4], P(None, None, 'band')
The draws below stay inside these ranges and needn't reach their ends.
Inputs may be any that keep to these rules, and one draw needn't show every extreme that they name: `column_map`: distinct grid columns, each numbered x * 192 + y; they are the 16384 columns nearest signed frequency (0, 0), that is with the smallest fx*fx + fy*fy, ties in any order. `block_index`: A block of the planes of the device that holds the entry. `block_atom`: with n the length of the pw axis and r = floor(2000 / n), an entry on pw device p names an atom a with (a - floor(p * 2000 / n) + 2 r) mod 2000 at most 5 r. Several entries may name one atom, and one block.
All inputs are finite; a program needn't handle non-finite values.
Results may differ from the reference program's by a relative error of at most 0.00031.
The reference program's roundings to bfloat16 on the way count: a program that leaves them out, or rounds other values in their place, can miss the bound.
Values may be sent and summed in bfloat16 or wider, within the bound.
No kernel may reach another device: no remote copies, remote signals or barrier semaphores. Data moves between devices by JAX's collectives and lax.ppermute only.
A program may use at most 128 MiB of HBM per device.

```python
import math
import jax
import jax.numpy as jnp
from jax import lax

NX = 192
NY = 192
NZ = 192
NCOL = 16384
KMAX = 73
NPROJ = 8
BLOCK = 128
NATOM = 2000
ENT_DEV = 512
BANDS = 4
NENT = 32768
BLK_DEV = 864
N_PW = 64


def draw_column_map(key, part):
    key = jax.random.fold_in(key, 11)
    first, second = jax.random.split(key)
    order = jax.random.permutation(first, NX * NY).astype(jnp.int32)
    xs = order // NY
    ys = order % NY
    freq_x = jnp.where(xs >= NX // 2, xs - NX, xs)
    freq_y = jnp.where(ys >= NY // 2, ys - NY, ys)
    radius_sq = freq_x * freq_x + freq_y * freq_y
    ranked = jnp.argsort(radius_sq, stable=True)
    chosen = order[ranked[:NCOL]]
    shuffle = jax.random.permutation(second, NCOL)
    return chosen[shuffle].astype(jnp.int32)


def draw_block_index(key, part):
    key = jax.random.fold_in(key, 5)
    values = jax.random.randint(key, (NENT,), 0, BLK_DEV, dtype=jnp.int32)
    position = jnp.arange(NENT, dtype=jnp.int32) % ENT_DEV
    values = jnp.where(position == 0, BLK_DEV - 1, jnp.where(position == 1, 0, values))
    return values.astype(jnp.int32)


def draw_block_atom(key, part):
    key = jax.random.fold_in(key, 7)
    entries = jnp.arange(NENT, dtype=jnp.int32)
    home = entries // ENT_DEV * NATOM // N_PW
    reach = NATOM // N_PW
    offset = jax.random.randint(key, (NENT,), -2 * reach, 3 * reach + 1, dtype=jnp.int32)
    atoms = (home + offset) % NATOM
    atoms = jnp.where(entries == 0, NATOM - 1, jnp.where(entries == 1, 0, atoms))
    return atoms.astype(jnp.int32)


def block_levels(key, extent, shards, low, largest):
    level, own = 1.0, jax.random.fold_in(key, 6)
    for axis_at, blocks in shards:
        steps = jnp.exp(jax.random.uniform(jax.random.fold_in(own, axis_at), (blocks,), jnp.float32, low / len(shards), largest / len(shards)))
        level = level * jnp.repeat(steps, extent[axis_at] // blocks).reshape([-1 if axis == axis_at else 1 for axis in range(len(extent))])
    return level


def gaussian(own_key, extent, spread, most, cuts=(), held_as=jnp.bfloat16):
    values = jax.random.normal(own_key, extent, jnp.float32) * spread
    if len(cuts) > 0:
        values = block_levels(own_key, extent, cuts, -0.22, 0.18) * values
    return jnp.clip(values, min=-most, max=most).astype(held_as)


def setup_inputs(seed: int = 0) -> dict:
    seeds = jax.random.split(jax.random.key(seed), 8)
    return {
        "orbitals": gaussian(seeds[0], (BANDS, 2, NZ, NCOL), 1.0, 6.0, ((0, 4), (3, 64))),
        "column_map": draw_column_map(jax.random.fold_in(seeds[7], 71), 0),
        "potential": jnp.clip(-1.5 + 2.5 * jax.random.uniform(seeds[2], (NZ, NX, NY), jnp.float32) ** block_levels(seeds[2], (NZ, NX, NY), ((0, 64),), -0.2, 0.2), -1.5, 1.0),
        "projectors": gaussian(seeds[3], (NENT, NPROJ, BLOCK), 0.1, 0.59765625, ((0, 64),)),
        "block_index": draw_block_index(jax.random.fold_in(seeds[7], 71), 0),
        "block_atom": draw_block_atom(jax.random.fold_in(seeds[7], 71), 0),
        "coupling": gaussian(seeds[6], (NATOM, NPROJ, NPROJ), 0.2, 1.2, (), jnp.float32),
    }


kinetic_unit = 0.5 * (2.0 * math.pi / 58.6) ** 2

def dft_table(length, sign):
    steps = jnp.arange(length, dtype=jnp.int32)
    product = steps[:, None] * steps[None, :] % length
    angles = product.astype(jnp.float32) * (2.0 * math.pi / length)
    cosines = jnp.cos(angles) / math.sqrt(length)
    sines = sign * jnp.sin(angles) / math.sqrt(length)
    table = jnp.stack([jnp.stack([cosines, sines], 1), jnp.stack([-sines, cosines], 1)], 0)
    return table.astype(jnp.bfloat16)

def signed_freq(index, length):
    return jnp.where(index >= length // 2, index - length, index)

def reference(orbitals, column_map, potential, projectors, block_index, block_atom, coupling):
    f32 = jnp.float32
    freq_x = signed_freq(column_map // NY, NX)
    freq_y = signed_freq(column_map % NY, NY)
    freq_z = signed_freq(jnp.arange(NZ, dtype=jnp.int32), NZ)
    radius_sq = freq_z[:, None] * freq_z[:, None] + (freq_x * freq_x + freq_y * freq_y)[None, :]
    sphere = radius_sq <= KMAX * KMAX
    kinetic = kinetic_unit * radius_sq.astype(f32)
    masked = jnp.where(sphere, orbitals, jnp.zeros_like(orbitals))
    fwd_z = dft_table(NZ, 1.0).astype(f32)
    fwd_y = dft_table(NY, 1.0).astype(f32)
    fwd_x = dft_table(NX, 1.0).astype(f32)
    back_z = dft_table(NZ, -1.0).astype(f32)
    back_y = dft_table(NY, -1.0).astype(f32)
    back_x = dft_table(NX, -1.0).astype(f32)
    global_block = block_index + jnp.arange(NENT, dtype=jnp.int32) // ENT_DEV * BLK_DEV
    nblocks = NZ * NX * NY // BLOCK
    proj_f = projectors.astype(f32)

    def one_band(band_data):
        zpass = jnp.einsum('czg,czdw->dwg', band_data.astype(f32), fwd_z).astype(jnp.bfloat16)
        grid = jnp.zeros((2, NZ, NX * NY), jnp.bfloat16).at[:, :, column_map].set(zpass)
        grid = grid.reshape(2, NZ, NX, NY)
        ydone = jnp.einsum('czxy,cydv->dzxv', grid.astype(f32), fwd_y).astype(jnp.bfloat16)
        real_space = jnp.einsum('czxy,cxdw->dzwy', ydone.astype(f32), fwd_x).astype(jnp.bfloat16)
        blocks = real_space.reshape(2, nblocks, BLOCK)
        picked = blocks[:, global_block, :].astype(f32)
        entry_correlation = jnp.einsum('cep,ejp->cej', picked, proj_f)
        correlation = jnp.zeros((2, NATOM, NPROJ), f32).at[:, block_atom].add(entry_correlation)
        weight = lax.optimization_barrier(jnp.sum(coupling[None] * correlation[:, :, None, :], -1)).astype(jnp.bfloat16)
        entry_weight = weight[:, block_atom].astype(f32)
        entry_terms = jnp.einsum('cej,ejp->cep', entry_weight, proj_f)
        nonlocal_part = jnp.zeros((2, nblocks, BLOCK), f32).at[:, global_block].add(entry_terms)
        nonlocal_part = nonlocal_part.reshape(2, NZ, NX, NY)
        h_real = (potential[None] * real_space.astype(f32) + nonlocal_part).astype(jnp.bfloat16)
        x_back = jnp.einsum('czxy,cxdw->dzwy', h_real.astype(f32), back_x).astype(jnp.bfloat16)
        y_back = jnp.einsum('czxy,cydv->dzxv', x_back.astype(f32), back_y)
        y_back = y_back.reshape(2, NZ, NX * NY)[:, :, column_map].astype(jnp.bfloat16)
        z_back = jnp.einsum('czg,czdw->dwg', y_back.astype(f32), back_z)
        result = kinetic[None] * band_data.astype(f32) + z_back
        return jnp.where(sphere[None], result, jnp.zeros_like(result))
    applied = lax.map(one_band, masked)
    masked_f = masked.astype(f32)
    high = lax.Precision.HIGHEST
    real_part = jnp.einsum('aczg,bczg->ab', masked_f, applied, precision=high)
    imag_part = jnp.einsum('azg,bzg->ab', masked_f[:, 0], applied[:, 1], precision=high) - jnp.einsum('azg,bzg->ab', masked_f[:, 1], applied[:, 0], precision=high)
    scale = 1.0 / (NZ * NCOL)
    subspace = jnp.stack([real_part, imag_part], 0) * scale
    return (applied, subspace)
```

```python
import math

import jax
import jax.numpy as jnp
import numpy as np
from jax import lax
from jax.experimental import pallas as pl
from jax.experimental.pallas import tpu as pltpu
from jax.sharding import PartitionSpec as P

KMAX = 73
BLOCK = 128
LANES = 128
BOX = 160
SLOTS = 256
kinetic_unit = 0.5 * (2.0 * math.pi / 58.6) ** 2
f32, bf16, i32 = jnp.float32, jnp.bfloat16, jnp.int32


def dft_table(length, sign):
    steps = np.arange(length, dtype=np.int32)
    product = steps[:, None] * steps[None, :] % length
    angles = product.astype(np.float32) * np.float32(2.0 * math.pi / length)
    root = np.float32(math.sqrt(length))
    cosines = np.cos(angles) / root
    sines = np.float32(sign) * np.sin(angles) / root
    return np.stack([np.stack([cosines, sines], 1), np.stack([-sines, cosines], 1)], 0).astype(np.float32)


def box_half(grid_x, grid_y, ncolumns):
    freq_x = np.arange(grid_x) - grid_x * (np.arange(grid_x) >= grid_x // 2)
    freq_y = np.arange(grid_y) - grid_y * (np.arange(grid_y) >= grid_y // 2)
    radius_sq = np.sort((freq_x[:, None] ** 2 + freq_y[None, :] ** 2).ravel())
    return int(math.isqrt(int(radius_sq[ncolumns - 1])))


def make_tables(grid_z, grid_x, grid_y, z_local, half):
    count = grid_z // z_local
    width = 2 * half + 1
    fwd_z, back_z = dft_table(grid_z, 1.0), dft_table(grid_z, -1.0)
    fwd_x, back_x = dft_table(grid_x, 1.0), dft_table(grid_x, -1.0)
    fwd_y, back_y = dft_table(grid_y, 1.0), dft_table(grid_y, -1.0)
    box_x = (np.arange(width) - half) % grid_x
    box_y = (np.arange(width) - half) % grid_y
    zf = np.zeros((count, 8, 2 * grid_z), np.float32)
    zb = np.zeros((2 * grid_z, count, 8), np.float32)
    for d in range(2):
        for plane in range(z_local):
            w = np.arange(count) * z_local + plane
            zf[:, d * z_local + plane, :] = fwd_z[:, :, d, w].reshape(2 * grid_z, count).T
            zb[:, :, d * z_local + plane] = back_z[d, w].reshape(count, 2 * grid_z).T
    yf = np.zeros((2, BOX, 2, 256), np.float32)
    yf[:, :width, :, :grid_y] = fwd_y[:, box_y]
    xf = np.zeros((2, 2 * grid_x, BOX), np.float32)
    order = np.concatenate([np.arange(0, grid_x, 2), np.arange(1, grid_x, 2)])
    for c in range(2):
        xf[c, :, :width] = fwd_x[c, box_x][:, :, order].reshape(width, 2 * grid_x).T
    xb = np.zeros((2, BOX, 2, grid_x), np.float32)
    for c in range(2):
        for d in range(2):
            xb[d, :width, c] = back_x[c, order][:, d, box_x].T
    yb = np.zeros((2, 256, 2, BOX), np.float32)
    yb[:, :grid_y, :, :width] = back_y[:, :, :, box_y]
    arrays = (
        zf.reshape(count * 8, -1), zb.reshape(2 * grid_z, -1), yf.reshape(2, BOX, 512), xf,
        xb.reshape(2 * BOX, 2 * grid_x), yb.transpose(2, 0, 1, 3),
    )
    return [jnp.asarray(a.astype(jnp.bfloat16)) for a in arrays]


def dot(a, b, dims=((1,), (0,))):
    return lax.dot_general(a, b, (dims, ((), ())), preferred_element_type=f32)


def split3(x):
    hi = x.astype(bf16)
    rest = x - hi.astype(f32)
    mid = rest.astype(bf16)
    low = (rest - mid.astype(f32)).astype(bf16)
    return hi, mid, low


def iota(shape, axis):
    return lax.broadcasted_iota(i32, shape, axis)


def ones_where(mask):
    return jnp.where(mask, 1.0, 0.0).astype(bf16)


def quotient(values, divisor):
    return jnp.floor((values.astype(f32) + 0.5) * (1.0 / divisor)).astype(i32)


def frequencies(columns, grid_x, grid_y):
    x = quotient(columns, grid_y)
    y = columns - x * grid_y
    return jnp.where(x >= grid_x // 2, x - grid_x, x), jnp.where(y >= grid_y // 2, y - grid_y, y)


def radius_rows(p_ref, cm_ref, grid_x, grid_y, grid_z):
    own = cm_ref[pl.ds(2 * p_ref[0], 2), :]
    freq_x, freq_y = frequencies(own, grid_x, grid_y)
    flat = freq_x * freq_x + freq_y * freq_y
    row = iota((2 * grid_z, LANES), 0)
    z = jnp.where(row >= grid_z, row - grid_z, row)
    freq_z = jnp.where(z >= grid_z // 2, z - grid_z, z)
    sq = freq_z * freq_z
    return [sq + flat[h : h + 1, :] for h in range(2)]


def build(sizes):
    (grid_z, grid_x, grid_y, z_local, count, bands, natoms, nproj, entries, half) = sizes
    pairs = grid_x // 2
    blocks = z_local * grid_x * grid_y // BLOCK
    plane_blocks = blocks // z_local
    reach = natoms // count
    chunks = entries // LANES
    cj = 2 * nproj
    nch = 2 * z_local
    steps = 4

    def block_rows(values):
        plane = quotient(values, plane_blocks)
        rest = values - plane * plane_blocks
        k = quotient(rest, 3)
        return plane * plane_blocks + (rest - 3 * k) * pairs + k

    def slots_of(values, p):
        start = p * natoms // count - 2 * reach
        t = values - start
        t = jnp.where(t < 0, t + natoms, t)
        return jnp.where(t >= natoms, t - natoms, t)

    def columns_of(rows):
        padded = jnp.concatenate([rows.astype(f32), jnp.zeros((8 - chunks, LANES), f32)], 0)
        return padded.T.astype(i32)

    def slot_onehot(at_ref, p):
        cols = columns_of(slots_of(at_ref[...], p))
        lane = iota((LANES, SLOTS), 1)
        return jnp.concatenate([ones_where(lane == cols[:, i : i + 1]) for i in range(chunks)], 0)

    def spread_projectors(proj_ref, pf_ref):
        pf_ref[...] = proj_ref[...].astype(f32).reshape(entries * nproj, BLOCK)

    def box_indices(cm_ref, xi_ref, yi_ref):
        freq_x, freq_y = frequencies(cm_ref[...], grid_x, grid_y)
        xi_ref[...] = freq_x + half
        yi_ref[...] = freq_y + half

    def to_columns(p_ref, cm_ref, orb_ref, tab_ref, out_ref):
        radius = radius_rows(p_ref, cm_ref, grid_x, grid_y, grid_z)
        parts = []
        for h in range(2):
            values = orb_ref[:, h * LANES : (h + 1) * LANES].astype(f32)
            parts.append(jnp.where(radius[h] <= KMAX * KMAX, values, 0.0).astype(bf16))
        z = dot(tab_ref[...], jnp.concatenate(parts, 1))
        out = [z[:, h * LANES : (h + 1) * LANES].reshape(count, 8, LANES) for h in range(2)]
        out_ref[...] = jnp.concatenate(out, 1).astype(bf16)

    def forward(p_ref, cm_ref, zr_ref, yf_ref, xf_ref, bi_ref, at_ref, proj_ref,
                rs_ref, win_ref, send_ref, xi_ref, yi_ref, acc_ref, pf_ref):
        p = p_ref[0]
        box_indices(cm_ref, xi_ref, yi_ref)
        acc_ref[...] = jnp.zeros_like(acc_ref)
        box_row = iota((BOX, LANES), 0)

        def add_columns(step, carry):
            xrows = xi_ref[pl.ds(pl.multiple_of(step * 2 * steps, 8), 2 * steps), :]
            yrows = yi_ref[pl.ds(pl.multiple_of(step * 2 * steps, 8), 2 * steps), :]
            left, right = [], []
            for s in range(steps):
                v = zr_ref[step * steps + s].astype(f32)
                for h in range(2):
                    r = 2 * s + h
                    hot = ones_where(box_row == xrows[r : r + 1, :]).reshape(BOX // 16, 16, LANES)
                    right.append(ones_where(box_row == yrows[r : r + 1, :]))
                    rows = []
                    for ch in range(nch):
                        one = v[h * 8 + ch : h * 8 + ch + 1, :]
                        wide = jnp.broadcast_to(one, (16, LANES)).astype(bf16)
                        rows.append((hot * wide[None]).reshape(BOX, LANES))
                    left.append(jnp.concatenate(rows, 0))
            acc_ref[...] += dot(jnp.concatenate(left, 1), jnp.concatenate(right, 1), ((1,), (1,)))
            return carry

        lax.fori_loop(0, count // steps, add_columns, 0)
        rows = z_local * BOX
        ydone = dot(acc_ref[0:rows, :].astype(bf16), yf_ref[0]) + dot(
            acc_ref[rows : 2 * rows, :].astype(bf16), yf_ref[1]
        )
        ydone = ydone.astype(bf16)
        lane = iota((pairs, LANES), 1)
        for plane in range(z_local):
            mine = ydone[plane * BOX : (plane + 1) * BOX]
            real = dot(xf_ref[0], mine[:, 0:256]) + dot(xf_ref[1], mine[:, 256:512])
            for d in range(2):
                even = real[d * grid_x : d * grid_x + pairs]
                odd = real[d * grid_x + pairs : (d + 1) * grid_x]
                turned = pltpu.roll(odd[:, 0:128], 64, 1)
                middle = jnp.where(lane < 64, even[:, 128:256], turned)
                last = jnp.where(lane < 64, turned, pltpu.roll(odd[:, 128:256], 64, 1))
                for t, piece in enumerate((even[:, 0:128], middle, last)):
                    at = plane * plane_blocks + t * pairs
                    rs_ref[at : at + pairs, d * BLOCK : (d + 1) * BLOCK] = piece.astype(bf16)
        spread_projectors(proj_ref, pf_ref)
        cols = columns_of(block_rows(bi_ref[...]))
        block_lane = iota((LANES, blocks), 1)
        hot = jnp.concatenate(
            [ones_where(block_lane == cols[:, i : i + 1]) for i in range(chunks)], 0
        )
        picked = dot(hot, rs_ref[...])
        select_row = iota((2 * BLOCK, LANES), 0)
        select_lane = iota((2 * BLOCK, LANES), 1)
        corr = jnp.zeros((entries, LANES), f32)
        for j in range(nproj):
            values = pf_ref[pl.ds(j, entries, stride=nproj), :]
            product = jnp.concatenate([values, values], 1) * picked
            hi = product.astype(bf16)
            low = (product - hi.astype(f32)).astype(bf16)
            target = jnp.where(select_row >= BLOCK, nproj + j, j)
            ones = ones_where(select_lane == target)
            corr = corr + (dot(hi, ones) + dot(low, ones))
        pieces = jnp.concatenate(split3(corr), 1)
        window = dot(pieces, slot_onehot(at_ref, p), ((0,), (0,)))
        window = window[0:cj] + window[LANES : LANES + cj] + window[2 * LANES : 2 * LANES + cj]
        win_ref[...] = window
        send_ref[...] = jnp.zeros_like(send_ref)
        home = p * natoms // count
        for s in range(1, 5):
            up = lax.rem(p + s, count)
            ahead = up * natoms // count - home
            ahead = jnp.where(ahead < 0, ahead + natoms, ahead)
            send_ref[up] = pltpu.roll(window, SLOTS - ahead, 1)[:, 0:LANES]
            down = lax.rem(p - s + count, count)
            send_ref[down] = window[:, 0:LANES]

    def backward(p_ref, cm_ref, xr_ref, win_ref, rs_ref, pot_ref, coup_ref, bi_ref, at_ref, proj_ref,
                 xb_ref, yb_ref, zall_ref, oall_ref, out_ref,
                 xi_ref, yi_ref, pf_ref, grid_ref, ret_ref, pot_first, pot_rest):
        p = p_ref[0]
        pot_first[...] = pot_ref[:, :, 0:LANES].reshape(z_local * grid_x, LANES)
        pot_rest[:, 0 : grid_y - LANES] = pot_ref[:, :, LANES:grid_y].reshape(
            z_local * grid_x, grid_y - LANES
        )
        home = p * natoms // count
        spread_projectors(proj_ref, pf_ref)
        total = win_ref[...]
        nothing = jnp.zeros((cj, LANES), f32)
        for s in range(1, 5):
            down = lax.rem(p - s + count, count)
            total = total + jnp.concatenate([xr_ref[down], nothing], 1)
            up = lax.rem(p + s, count)
            ahead = up * natoms // count - home
            ahead = jnp.where(ahead < 0, ahead + natoms, ahead)
            total = total + pltpu.roll(jnp.concatenate([xr_ref[up], nothing], 1), ahead, 1)
        start = home - 2 * reach
        atom = start + iota((natoms, SLOTS), 1)
        atom = jnp.where(atom < 0, atom + natoms, atom)
        atom = jnp.where(atom >= natoms, atom - natoms, atom)
        select = ones_where(atom == iota((natoms, SLOTS), 0))
        near = dot(jnp.concatenate(split3(coup_ref[...]), 0), select)
        square = nproj * nproj
        near = near[0:square] + near[square : 2 * square] + near[2 * square : 3 * square]
        near = near.reshape(nproj, nproj, SLOTS)
        weight = jnp.concatenate(
            [jnp.sum(near * total[c * nproj : (c + 1) * nproj][None], 1) for c in range(2)], 0
        ).astype(bf16)
        ent_weight = dot(slot_onehot(at_ref, p), weight, ((1,), (1,)))
        terms = [jnp.zeros((entries, BLOCK), f32) for _ in range(2)]
        for j in range(nproj):
            values = pf_ref[pl.ds(j, entries, stride=nproj), :]
            for c in range(2):
                terms[c] = terms[c] + ent_weight[:, c * nproj + j : c * nproj + j + 1] * values
        pieces = jnp.concatenate(split3(jnp.concatenate(terms, 1)), 1)
        rows = block_rows(bi_ref[...])
        block_row = iota((blocks, LANES), 0)
        hot = jnp.concatenate(
            [ones_where(block_row == rows[i : i + 1, :]) for i in range(chunks)], 1
        )
        nonlocal_part = dot(hot, pieces)
        nonlocal_part = (
            nonlocal_part[:, 0:256] + nonlocal_part[:, 256:512] + nonlocal_part[:, 512:768]
        )
        lane = iota((pairs, LANES), 1)
        backs = [[], []]
        for plane in range(z_local):
            at = plane * plane_blocks
            even, odd = (
                [
                    part[pl.ds(plane * grid_x + parity, pairs, stride=2), :]
                    for part in (pot_first, pot_rest)
                ]
                for parity in range(2)
            )
            turned = pltpu.roll(odd[0], 64, 1)
            pot = (
                even[0],
                jnp.where(lane < 64, even[1], turned),
                jnp.where(lane < 64, turned, pltpu.roll(odd[1], 64, 1)),
            )
            stacked = []
            for c in range(2):
                h = []
                for t in range(3):
                    own = slice(at + t * pairs, at + (t + 1) * pairs)
                    lanes = slice(c * BLOCK, (c + 1) * BLOCK)
                    h.append(pot[t] * rs_ref[own, lanes].astype(f32) + nonlocal_part[own, lanes])
                swung = pltpu.roll(h[2], 64, 1)
                stacked.append(jnp.concatenate([h[0], jnp.where(lane < 64, h[1], 0.0)], 1))
                stacked.append(
                    jnp.concatenate(
                        [
                            jnp.where(lane < 64, pltpu.roll(h[1], 64, 1), swung),
                            jnp.where(lane < 64, swung, 0.0),
                        ],
                        1,
                    )
                )
            x_back = dot(xb_ref[...], jnp.concatenate(stacked, 0).astype(bf16)).astype(bf16)
            for c in range(2):
                backs[c].append(x_back[c * BOX : (c + 1) * BOX])
        backs = [jnp.concatenate(b, 0) for b in backs]
        rows_d = z_local * BOX
        for d in range(2):
            y_back = dot(backs[0], yb_ref[d, 0]) + dot(backs[1], yb_ref[d, 1])
            grid_ref[d * rows_d : (d + 1) * rows_d, :] = y_back.astype(bf16)
        box_indices(cm_ref, xi_ref, yi_ref)
        box_row = iota((BOX, LANES), 0)
        blank = jnp.zeros((8 - nch, LANES), f32)

        def take_columns(step, carry):
            base = pl.multiple_of(step * 8, 8)
            xrows = xi_ref[pl.ds(base, 8), :]
            yrows = yi_ref[pl.ds(base, 8), :]
            sums = list(carry)
            for s in range(4):
                hot_y = jnp.concatenate(
                    [ones_where(box_row == yrows[2 * s + h : 2 * s + h + 1, :]) for h in range(2)], 1
                )
                taken = dot(grid_ref[...], hot_y)
                halves, swapped = [], []
                for h in range(2):
                    mask = box_row == xrows[2 * s + h : 2 * s + h + 1, :]
                    rows = []
                    for ch in range(nch):
                        part = taken[ch * BOX : (ch + 1) * BOX, h * LANES : (h + 1) * LANES]
                        row = jnp.sum(jnp.where(mask, part, 0.0), 0, keepdims=True)
                        rows.append(row)
                    halves.append(jnp.concatenate(rows + [blank], 0))
                    other = rows[z_local:] + [-r for r in rows[:z_local]]
                    swapped.append(jnp.concatenate(other + [blank], 0))
                ret = jnp.concatenate(halves, 0)
                cross = jnp.concatenate(swapped, 0)
                ret_ref[step * 4 + s] = ret
                for m in range(bands):
                    other = zall_ref[m, step * 4 + s].astype(f32)
                    sums[m] = sums[m] + other * ret
                    sums[bands + m] = sums[bands + m] + other * cross
            return tuple(sums)

        zero = jnp.zeros((16, LANES), f32)
        sums = lax.fori_loop(0, count // 4, take_columns, (zero,) * (2 * bands))
        radius = radius_rows(p_ref, cm_ref, grid_x, grid_y, grid_z)
        band = p_ref[1]
        kin = [jnp.zeros((1, LANES), f32) for _ in range(2 * bands)]
        for h in range(2):
            lanes = slice(h * LANES, (h + 1) * LANES)
            own = oall_ref[band, :, lanes].astype(f32)
            kinetic = jnp.where(radius[h] <= KMAX * KMAX, kinetic_unit * radius[h].astype(f32), 0.0)
            own = kinetic * own
            for m in range(bands):
                other = oall_ref[m, :, lanes].astype(f32)
                kin[m] = kin[m] + jnp.sum(other * own, 0, keepdims=True)
                kin[bands + m] = kin[bands + m] + jnp.sum(
                    other[:grid_z] * own[grid_z:] - other[grid_z:] * own[:grid_z], 0, keepdims=True
                )
        lane = iota((1, LANES), 1)
        row = jnp.zeros((1, LANES), f32)
        for n in range(2 * bands):
            value = jnp.sum(sums[n], 0, keepdims=True) + kin[n]
            value = jnp.sum(value, 1, keepdims=True)
            for k, piece in enumerate(split3(value)):
                row = jnp.where(lane == 2 * bands * k + n, piece.astype(f32), row)
        sub = iota((16, LANES), 0)
        carried = jnp.where(sub == nch, jnp.broadcast_to(row, (16, LANES)), 0.0)
        out_ref[...] = (ret_ref[...] + carried[None]).astype(bf16)

    def finish(p_ref, cm_ref, orb_ref, rr_ref, tab_ref, applied_ref, sub_ref):
        radius = radius_rows(p_ref, cm_ref, grid_x, grid_y, grid_z)
        got = rr_ref[...].astype(f32)
        right = jnp.concatenate(
            [got[:, h * 8 : (h + 1) * 8].reshape(count * 8, LANES) for h in range(2)], 1
        ).astype(bf16)
        z_back = dot(tab_ref[...], right)
        for h in range(2):
            lanes = slice(h * LANES, (h + 1) * LANES)
            values = orb_ref[:, lanes].astype(f32)
            result = kinetic_unit * radius[h].astype(f32) * values + z_back[:, lanes]
            applied_ref[:, lanes] = jnp.where(radius[h] <= KMAX * KMAX, result, 0.0)
        summed = jnp.sum(got[:, 0:8], 0)
        summed = summed + (
            pltpu.roll(summed, LANES - 2 * bands, 1) + pltpu.roll(summed, LANES - 4 * bands, 1)
        )
        sub_ref[...] = summed * (1.0 / (grid_z * count * 2 * LANES))

    return to_columns, forward, backward, finish


def call(kernel, out_shape, n_scalar, n_in, scratch=()):
    smem = pl.BlockSpec(memory_space=pltpu.SMEM)
    vmem = pl.BlockSpec(memory_space=pltpu.VMEM)
    multiple = isinstance(out_shape, (list, tuple))
    return pl.pallas_call(
        kernel,
        out_shape=out_shape,
        in_specs=[smem] * n_scalar + [vmem] * n_in,
        out_specs=[vmem] * len(out_shape) if multiple else vmem,
        scratch_shapes=list(scratch),
        compiler_params=pltpu.CompilerParams(vmem_limit_bytes=56 * 1024 * 1024),
    )


def per_device(orbitals, column_map, potential, projectors, block_index, block_atom, coupling):
    _, _, grid_z, col_local = orbitals.shape
    z_local, grid_x, grid_y = potential.shape
    natoms, nproj = coupling.shape[0], coupling.shape[1]
    entries = block_index.shape[0]
    count, bands = lax.axis_size("pw"), lax.axis_size("band")
    ncolumns = column_map.shape[0]
    half = box_half(grid_x, grid_y, ncolumns)
    zf, zb, yf, xf, xb, yb = make_tables(grid_z, grid_x, grid_y, z_local, half)
    sizes = (grid_z, grid_x, grid_y, z_local, count, bands, natoms, nproj, entries, half)
    to_columns, forward, backward, finish = build(sizes)
    shape = jax.ShapeDtypeStruct
    blocks = z_local * grid_x * grid_y // BLOCK
    cj = 2 * nproj

    place = jnp.stack([lax.axis_index("pw"), lax.axis_index("band")]).astype(i32)
    cm = column_map.reshape(ncolumns // LANES, LANES)
    orb = orbitals.reshape(2 * grid_z, col_local)
    bi = block_index.reshape(entries // LANES, LANES)
    at = block_atom.reshape(entries // LANES, LANES)
    coup = coupling.reshape(natoms, nproj * nproj).T
    packet = (count, 16, LANES)

    sent = call(to_columns, shape(packet, bf16), 1, 3)(place, cm, orb, zf)
    planes = lax.all_to_all(sent, "pw", split_axis=0, concat_axis=0, tiled=True)
    index_scratch = [pltpu.VMEM(cm.shape, i32), pltpu.VMEM(cm.shape, i32)]
    pf_scratch = pltpu.VMEM((entries * nproj, BLOCK), f32)
    real_space, window, to_send = call(
        forward,
        (shape((blocks, 2 * BLOCK), bf16), shape((cj, SLOTS), f32), shape((count, cj, LANES), f32)),
        1, 7,
        index_scratch + [pltpu.VMEM((2 * z_local * BOX, BOX), f32), pf_scratch],
    )(place, cm, planes, yf, xf, bi, at, projectors)
    other = lax.all_to_all(to_send, "pw", split_axis=0, concat_axis=0, tiled=True)
    all_planes = lax.all_gather(planes, "band", axis=0, tiled=False)
    all_orb = lax.all_gather(orb, "band", axis=0, tiled=False)
    back = call(
        backward, shape(packet, bf16), 1, 13,
        index_scratch
        + [pf_scratch, pltpu.VMEM((2 * z_local * BOX, BOX), bf16), pltpu.VMEM(packet, f32)]
        + [pltpu.VMEM((z_local * grid_x, LANES), f32)] * 2,
    )(place, cm, other, window, real_space, potential, coup, bi, at, projectors, xb, yb, all_planes, all_orb)
    returned = lax.all_to_all(back, "pw", split_axis=0, concat_axis=0, tiled=True)
    applied, sums = call(
        finish, (shape((2 * grid_z, col_local), f32), shape((8, LANES), f32)), 1, 4
    )(place, cm, orb, returned, zb)
    applied = applied.reshape(1, 2, grid_z, col_local)
    subspace = sums[2 * z_local, : 2 * bands].reshape(2, bands, 1)
    return applied, subspace


def solution(mesh):
    in_specs = (
        P("band", None, None, "pw"),
        P(),
        P("pw", None, None),
        P("pw", None, None),
        P("pw"),
        P("pw"),
        P(),
    )
    out_specs = (P("band", None, None, "pw"), P(None, None, "band"))
    return jax.shard_map(
        per_device, mesh=mesh, in_specs=in_specs, out_specs=out_specs, check_vma=False
    )
```

```python
import math

import jax
import jax.numpy as jnp
import numpy as np
from jax import lax
from jax.experimental import pallas as pl
from jax.experimental.pallas import tpu as pltpu
from jax.sharding import PartitionSpec as P

KMAX = 73
BLOCK = 128
LANES = 128
VMEM_MIB, ALL_MIB = 52, 58
MAIN, TAIL = 80, 16
PACK = MAIN + TAIL
SLOTS = 256
kinetic_unit = 0.5 * (2.0 * math.pi / 58.6) ** 2
f32, bf16, i32 = jnp.float32, jnp.bfloat16, jnp.int32


def dft_table(length, sign):
    steps = np.arange(length, dtype=np.int32)
    product = steps[:, None] * steps[None, :] % length
    angles = product.astype(np.float32) * np.float32(2.0 * math.pi / length)
    root = np.float32(math.sqrt(length))
    cosines = np.cos(angles) / root
    sines = np.float32(sign) * np.sin(angles) / root
    return np.stack([np.stack([cosines, sines], 1), np.stack([-sines, cosines], 1)], 0).astype(np.float32)


def box_half(grid_x, grid_y, ncolumns):
    freq_x = np.arange(grid_x) - grid_x * (np.arange(grid_x) >= grid_x // 2)
    freq_y = np.arange(grid_y) - grid_y * (np.arange(grid_y) >= grid_y // 2)
    radius_sq = np.sort((freq_x[:, None] ** 2 + freq_y[None, :] ** 2).ravel())
    return int(math.isqrt(int(radius_sq[ncolumns - 1])))


def make_tables(grid_z, grid_x, grid_y, z_local, half):
    count = grid_z // z_local
    width = 2 * half + 1
    fwd_z, back_z = dft_table(grid_z, 1.0), dft_table(grid_z, -1.0)
    fwd_x, back_x = dft_table(grid_x, 1.0), dft_table(grid_x, -1.0)
    fwd_y, back_y = dft_table(grid_y, 1.0), dft_table(grid_y, -1.0)
    box_x = (np.arange(width) - half) % grid_x
    box_y = (np.arange(width) - half) % grid_y
    zf = np.zeros((count, 8, 2 * grid_z), np.float32)
    zb = np.zeros((2 * grid_z, count, 8), np.float32)
    for d in range(2):
        for plane in range(z_local):
            w = np.arange(count) * z_local + plane
            zf[:, d * z_local + plane, :] = fwd_z[:, :, d, w].reshape(2 * grid_z, count).T
            zb[:, :, d * z_local + plane] = back_z[d, w].reshape(count, 2 * grid_z).T
    split = LANES
    more = width - split
    pair = [np.arange(par, width, 2) for par in range(2)]
    beyond = [np.arange(split + par, width, 2) for par in range(2)]
    yf = np.zeros((2, split, 2, 256), np.float32)
    yf[:, :, :, :grid_y] = fwd_y[:, box_y[:split]]
    yft = np.zeros((2, 2, TAIL, 2, 256), np.float32)
    xf = np.zeros((2 * grid_x, 2, 2, MAIN), np.float32)
    xb = np.zeros((2, 2, MAIN, 2, grid_x), np.float32)
    order = np.concatenate([np.arange(0, grid_x, 2), np.arange(1, grid_x, 2)])
    yb = np.zeros((2, 256, 2, split), np.float32)
    yb[:, :grid_y] = back_y[:, :, :, box_y[:split]]
    ybt = np.zeros((2, 2, 2, TAIL, 256), np.float32)
    for par in range(2):
        xs, ys = box_x[pair[par]], box_y[beyond[par]]
        yft[:, par, : len(ys), :, :grid_y] = fwd_y[:, ys]
        for c in range(2):
            xf[:, c, par, : len(xs)] = fwd_x[c, xs][:, :, order].reshape(len(xs), 2 * grid_x).T
            for d in range(2):
                xb[d, par, : len(xs), c] = back_x[c, order][:, d, xs].T
                ybt[c, d, par, : len(ys), :grid_y] = back_y[c, :, d, ys]
    arrays = (
        zf.reshape(count * 8, -1), zb.reshape(2 * grid_z, -1), yf.reshape(2 * split, 512),
        yft.reshape(4 * TAIL, 512), xf.reshape(2 * grid_x, 4 * MAIN), xb.reshape(4 * MAIN, 2 * grid_x),
        yb.reshape(2, 256, 2 * split), ybt.reshape(2, 4 * TAIL, 256),
    )
    reach_x = math.isqrt((half + 1) ** 2 - 1 - (split - half) ** 2)
    assert (half + reach_x) // 2 < 64 and (more + 1) // 2 <= TAIL and half + 1 <= MAIN
    return [jnp.asarray(a.astype(jnp.bfloat16)) for a in arrays]


def dot(a, b, dims=((1,), (0,))):
    return lax.dot_general(a, b, (dims, ((), ())), preferred_element_type=f32)


def split3(x):
    hi = x.astype(bf16)
    rest = x - hi.astype(f32)
    mid = rest.astype(bf16)
    low = (rest - mid.astype(f32)).astype(bf16)
    return hi, mid, low


def iota(shape, axis):
    return lax.broadcasted_iota(i32, shape, axis)


def ones_where(mask):
    return jnp.where(mask, 1.0, 0.0).astype(bf16)


def quotient(values, divisor):
    return jnp.floor((values.astype(f32) + 0.5) * (1.0 / divisor)).astype(i32)


def frequencies(columns, grid_x, grid_y):
    x = quotient(columns, grid_y)
    y = columns - x * grid_y
    return jnp.where(x >= grid_x // 2, x - grid_x, x), jnp.where(y >= grid_y // 2, y - grid_y, y)


def radius_rows(p, cm_ref, grid_x, grid_y, grid_z):
    own = cm_ref[pl.ds(2 * p, 2), :]
    freq_x, freq_y = frequencies(own, grid_x, grid_y)
    flat = freq_x * freq_x + freq_y * freq_y
    row = iota((2 * grid_z, LANES), 0)
    z = jnp.where(row >= grid_z, row - grid_z, row)
    freq_z = jnp.where(z >= grid_z // 2, z - grid_z, z)
    sq = freq_z * freq_z
    return [sq + flat[h : h + 1, :] for h in range(2)]


def build(sizes):
    (grid_z, grid_x, grid_y, z_local, count, bands, natoms, nproj, entries, half) = sizes
    pairs = grid_x // 2
    blocks = z_local * grid_x * grid_y // BLOCK
    plane_blocks = blocks // z_local
    reach = natoms // count
    chunks = entries // LANES
    cj = 2 * nproj
    nch = 2 * z_local
    steps = 16
    gsteps = 8
    rows_c = z_local * PACK

    def block_rows(values):
        plane = quotient(values, plane_blocks)
        rest = values - plane * plane_blocks
        k = quotient(rest, 3)
        return plane * plane_blocks + (rest - 3 * k) * pairs + k

    def slots_of(values, p):
        start = p * natoms // count - 2 * reach
        t = values - start
        t = jnp.where(t < 0, t + natoms, t)
        return jnp.where(t >= natoms, t - natoms, t)

    def columns_of(rows):
        padded = jnp.concatenate([rows.astype(f32), jnp.zeros((8 - chunks, LANES), f32)], 0)
        return padded.T.astype(i32)

    def slot_onehot(at_ref, p):
        cols = columns_of(slots_of(at_ref[...], p))
        lane = iota((LANES, SLOTS), 1)
        return jnp.concatenate([ones_where(lane == cols[:, i : i + 1]) for i in range(chunks)], 0)

    def box_indices(cm_ref, row_ref, lane_ref):
        freq_x, freq_y = frequencies(cm_ref[...], grid_x, grid_y)
        x, y = freq_x + half, freq_y + half
        pair, parity, more = x >> 1, x & 1, y - LANES
        row_ref[...] = jnp.where(more >= 0, MAIN + (more >> 1), pair)
        lane_ref[...] = jnp.where(
            more >= 0, (more & 1) * LANES + parity * 64 + pair, parity * LANES + y
        )

    def near_coupling(p, coup):
        start = p * natoms // count - 2 * reach
        atom = start + iota((natoms, SLOTS), 1)
        atom = jnp.where(atom < 0, atom + natoms, atom)
        atom = jnp.where(atom >= natoms, atom - natoms, atom)
        select = ones_where(atom == iota((natoms, SLOTS), 0))
        near = dot(jnp.concatenate(split3(coup()[...]), 0), select)
        square = nproj * nproj
        return near[0:square] + near[square : 2 * square] + near[2 * square : 3 * square]

    def to_columns(cm, orb, table, out_ref):
        p = lax.axis_index("pw")
        radius = radius_rows(p, cm(), grid_x, grid_y, grid_z)
        orb_ref = orb()
        parts = []
        for h in range(2):
            values = orb_ref[:, h * LANES : (h + 1) * LANES].astype(f32)
            parts.append(jnp.where(radius[h] <= KMAX * KMAX, values, 0.0).astype(bf16))
        z = dot(table()[...], jnp.concatenate(parts, 1))
        out = [z[:, h * LANES : (h + 1) * LANES].reshape(count, 8, LANES) for h in range(2)]
        out_ref[...] = jnp.concatenate(out, 1).astype(bf16)

    def forward(cm, zr_ref, yf, yft, xf, bi, at, proj, coup,
                rs_ref, win_ref, send_ref, near_ref, xi_ref, yi_ref, acc_ref, pf_ref):
        p = lax.axis_index("pw")
        box_indices(cm(), xi_ref, yi_ref)
        acc_ref[...] = jnp.zeros_like(acc_ref)
        pack_row = iota((PACK, LANES), 0)
        pack_lane = iota((256, LANES), 0)

        def add_columns(step, carry):
            xrows = xi_ref[pl.ds(pl.multiple_of(step * 2 * steps, 8), 2 * steps), :]
            yrows = yi_ref[pl.ds(pl.multiple_of(step * 2 * steps, 8), 2 * steps), :]
            left, right = [], []
            for s in range(steps):
                v = zr_ref[step * steps + s].astype(f32)
                for h in range(2):
                    r = 2 * s + h
                    hot = ones_where(pack_row == xrows[r : r + 1, :]).reshape(PACK // 16, 16, LANES)
                    right.append(ones_where(pack_lane == yrows[r : r + 1, :]))
                    rows = []
                    for ch in range(nch):
                        one = v[h * 8 + ch : h * 8 + ch + 1, :]
                        wide = jnp.broadcast_to(one, (16, LANES)).astype(bf16)
                        rows.append((hot * wide[None]).reshape(PACK, LANES))
                    left.append(jnp.concatenate(rows, 0))
            acc_ref[...] += dot(jnp.concatenate(left, 1), jnp.concatenate(right, 1), ((1,), (1,)))
            return carry

        lax.fori_loop(0, count // steps, add_columns, 0)
        yf_ref, yft_ref, xf_ref = yf(), yft(), xf()
        main, tails = [], []
        for plane in range(z_local):
            starts = [c * rows_c + plane * PACK for c in range(2)]
            for par in range(2):
                lanes = slice(par * LANES, (par + 1) * LANES)
                main.append(jnp.concatenate([acc_ref[r : r + MAIN, lanes] for r in starts], 1))
            tails.append(
                jnp.concatenate(
                    [
                        acc_ref[r + MAIN : r + PACK, par * LANES : (par + 1) * LANES]
                        for r in starts
                        for par in range(2)
                    ],
                    0,
                ).astype(bf16)
            )
        ydone = dot(jnp.concatenate(main, 0).astype(bf16), yf_ref[...])
        lane = iota((pairs, LANES), 1)
        for plane in range(z_local):
            more = dot(tails[plane], yft_ref[...], ((0,), (0,)))
            mine = []
            for par in range(2):
                r = (plane * 2 + par) * MAIN
                mine.append(ydone[r : r + 64] + more[par * 64 : (par + 1) * 64])
                mine.append(ydone[r + 64 : r + MAIN])
            mine = jnp.concatenate(mine, 0).astype(bf16)
            real = dot(xf_ref[...], jnp.concatenate([mine[:, 0:256], mine[:, 256:512]], 0))
            for d in range(2):
                even = real[d * grid_x : d * grid_x + pairs]
                odd = real[d * grid_x + pairs : (d + 1) * grid_x]
                turned = pltpu.roll(odd[:, 0:128], 64, 1)
                middle = jnp.where(lane < 64, even[:, 128:256], turned)
                last = jnp.where(lane < 64, turned, pltpu.roll(odd[:, 128:256], 64, 1))
                for t, piece in enumerate((even[:, 0:128], middle, last)):
                    own = plane * plane_blocks + t * pairs
                    rs_ref[own : own + pairs, d * BLOCK : (d + 1) * BLOCK] = piece.astype(bf16)
        near_ref[...] = near_coupling(p, coup)
        pf_ref[...] = proj()[...].astype(f32)
        cols = columns_of(block_rows(bi()[...]))
        block_lane = iota((LANES, blocks), 1)
        hot = jnp.concatenate(
            [ones_where(block_lane == cols[:, i : i + 1]) for i in range(chunks)], 0
        )
        picked = dot(hot, rs_ref[...])
        select_row = iota((2 * BLOCK, LANES), 0)
        select_lane = iota((2 * BLOCK, LANES), 1)
        corr = jnp.zeros((entries, LANES), f32)
        for j in range(nproj):
            values = pf_ref[pl.ds(j, entries, stride=nproj), :]
            product = jnp.concatenate([values, values], 1) * picked
            hi = product.astype(bf16)
            low = (product - hi.astype(f32)).astype(bf16)
            target = jnp.where(select_row >= BLOCK, nproj + j, j)
            ones = ones_where(select_lane == target)
            corr = corr + (dot(hi, ones) + dot(low, ones))
        pieces = jnp.concatenate(split3(corr), 1)
        window = dot(pieces, slot_onehot(at(), p), ((0,), (0,)))
        window = window[0:cj] + window[LANES : LANES + cj] + window[2 * LANES : 2 * LANES + cj]
        win_ref[...] = window
        send_ref[...] = jnp.zeros_like(send_ref)
        home = p * natoms // count
        for s in range(1, 5):
            up = lax.rem(p + s, count)
            ahead = up * natoms // count - home
            ahead = jnp.where(ahead < 0, ahead + natoms, ahead)
            send_ref[up] = pltpu.roll(window, SLOTS - ahead, 1)[:, 0:LANES]
            down = lax.rem(p - s + count, count)
            send_ref[down] = window[:, 0:LANES]

    def backward(cm, xr_ref, win_ref, rs_ref, potential, near_ref, bi, at, proj,
                 xb, yb, ybt, zall, oall, out_ref,
                 xi_ref, yi_ref, pf_ref, grid_ref, ret_ref, pot_first, pot_rest):
        p = lax.axis_index("pw")
        home = p * natoms // count
        total = win_ref[...]
        nothing = jnp.zeros((cj, LANES), f32)
        for s in range(1, 5):
            down = lax.rem(p - s + count, count)
            total = total + jnp.concatenate([xr_ref[down], nothing], 1)
            up = lax.rem(p + s, count)
            ahead = up * natoms // count - home
            ahead = jnp.where(ahead < 0, ahead + natoms, ahead)
            total = total + pltpu.roll(jnp.concatenate([xr_ref[up], nothing], 1), ahead, 1)
        near = near_ref[...]
        near = near.reshape(nproj, nproj, SLOTS)
        weight = jnp.concatenate(
            [jnp.sum(near * total[c * nproj : (c + 1) * nproj][None], 1) for c in range(2)], 0
        ).astype(bf16)
        pf_ref[...] = proj()[...].astype(f32)
        ent_weight = dot(slot_onehot(at(), p), weight, ((1,), (1,)))
        terms = [jnp.zeros((entries, BLOCK), f32) for _ in range(2)]
        for j in range(nproj):
            values = pf_ref[pl.ds(j, entries, stride=nproj), :]
            for c in range(2):
                terms[c] = terms[c] + ent_weight[:, c * nproj + j : c * nproj + j + 1] * values
        pieces = jnp.concatenate(split3(jnp.concatenate(terms, 1)), 1)
        rows = block_rows(bi()[...])
        block_row = iota((blocks, LANES), 0)
        hot = jnp.concatenate(
            [ones_where(block_row == rows[i : i + 1, :]) for i in range(chunks)], 1
        )
        nonlocal_part = dot(hot, pieces)
        nonlocal_part = (
            nonlocal_part[:, 0:256] + nonlocal_part[:, 256:512] + nonlocal_part[:, 512:768]
        )
        pot_ref = potential()
        pot_first[...] = pot_ref[:, :, 0:LANES].reshape(z_local * grid_x, LANES)
        pot_rest[:, 0 : grid_y - LANES] = pot_ref[:, :, LANES:grid_y].reshape(
            z_local * grid_x, grid_y - LANES
        )
        xb_ref, yb_ref, ybt_ref = xb(), yb(), ybt()
        lane = iota((pairs, LANES), 1)
        backs = [[], []]
        for plane in range(z_local):
            first = plane * plane_blocks
            even, odd = (
                [
                    part[pl.ds(plane * grid_x + parity, pairs, stride=2), :]
                    for part in (pot_first, pot_rest)
                ]
                for parity in range(2)
            )
            turned = pltpu.roll(odd[0], 64, 1)
            pot = (
                even[0],
                jnp.where(lane < 64, even[1], turned),
                jnp.where(lane < 64, turned, pltpu.roll(odd[1], 64, 1)),
            )
            stacked = []
            for c in range(2):
                h = []
                for t in range(3):
                    own = slice(first + t * pairs, first + (t + 1) * pairs)
                    lanes = slice(c * BLOCK, (c + 1) * BLOCK)
                    h.append(pot[t] * rs_ref[own, lanes].astype(f32) + nonlocal_part[own, lanes])
                swung = pltpu.roll(h[2], 64, 1)
                stacked.append(jnp.concatenate([h[0], jnp.where(lane < 64, h[1], 0.0)], 1))
                stacked.append(
                    jnp.concatenate(
                        [
                            jnp.where(lane < 64, pltpu.roll(h[1], 64, 1), swung),
                            jnp.where(lane < 64, swung, 0.0),
                        ],
                        1,
                    )
                )
            x_back = dot(xb_ref[...], jnp.concatenate(stacked, 0).astype(bf16)).astype(bf16)
            tail = jnp.zeros((4 * TAIL, LANES), f32)
            for c in range(2):
                mine = x_back[c * 2 * MAIN : (c + 1) * 2 * MAIN]
                backs[c].append(mine)
                near_rows = jnp.concatenate([mine[0:64], mine[MAIN : MAIN + 64]], 0)
                tail = tail + dot(ybt_ref[c], near_rows, ((1,), (1,)))
            for d in range(2):
                for par in range(2):
                    r = d * rows_c + plane * PACK + MAIN
                    own = (2 * d + par) * TAIL
                    grid_ref[r : r + TAIL, par * LANES : (par + 1) * LANES] = tail[
                        own : own + TAIL
                    ].astype(bf16)
        y_back = dot(jnp.concatenate(backs[0], 0), yb_ref[0]) + dot(
            jnp.concatenate(backs[1], 0), yb_ref[1]
        )
        for plane in range(z_local):
            for par in range(2):
                own = (plane * 2 + par) * MAIN
                for d in range(2):
                    r = d * rows_c + plane * PACK
                    grid_ref[r : r + MAIN, par * LANES : (par + 1) * LANES] = y_back[
                        own : own + MAIN, d * LANES : (d + 1) * LANES
                    ].astype(bf16)
        cm_ref, zall_ref = cm(), zall()
        box_indices(cm_ref, xi_ref, yi_ref)
        pack_row = iota((PACK, LANES), 0)
        pack_lane = iota((256, LANES), 0)
        blank = jnp.zeros((8 - nch, LANES), f32)

        def take_columns(step, carry):
            base = pl.multiple_of(step * 2 * gsteps, 8)
            xrows = xi_ref[pl.ds(base, 2 * gsteps), :]
            yrows = yi_ref[pl.ds(base, 2 * gsteps), :]
            sums = list(carry)
            for s in range(gsteps):
                hot_y = jnp.concatenate(
                    [ones_where(pack_lane == yrows[2 * s + h : 2 * s + h + 1, :]) for h in range(2)], 1
                )
                taken = dot(grid_ref[...], hot_y)
                halves, swapped = [], []
                for h in range(2):
                    mask = pack_row == xrows[2 * s + h : 2 * s + h + 1, :]
                    rows = []
                    for ch in range(nch):
                        part = taken[ch * PACK : (ch + 1) * PACK, h * LANES : (h + 1) * LANES]
                        row = jnp.sum(jnp.where(mask, part, 0.0), 0, keepdims=True)
                        rows.append(row)
                    halves.append(jnp.concatenate(rows + [blank], 0))
                    other = rows[z_local:] + [-r for r in rows[:z_local]]
                    swapped.append(jnp.concatenate(other + [blank], 0))
                ret = jnp.concatenate(halves, 0)
                cross = jnp.concatenate(swapped, 0)
                ret_ref[step * gsteps + s] = ret
                for m in range(bands):
                    other = zall_ref[m, step * gsteps + s].astype(f32)
                    sums[m] = sums[m] + other * ret
                    sums[bands + m] = sums[bands + m] + other * cross
            return tuple(sums)

        zero = jnp.zeros((16, LANES), f32)
        sums = lax.fori_loop(0, count // gsteps, take_columns, (zero,) * (2 * bands))
        radius = radius_rows(p, cm_ref, grid_x, grid_y, grid_z)
        band = lax.axis_index("band")
        oall_ref = oall()
        kin = [jnp.zeros((1, LANES), f32) for _ in range(2 * bands)]
        for h in range(2):
            lanes = slice(h * LANES, (h + 1) * LANES)
            own = oall_ref[band, :, lanes].astype(f32)
            kinetic = jnp.where(radius[h] <= KMAX * KMAX, kinetic_unit * radius[h].astype(f32), 0.0)
            own = kinetic * own
            for m in range(bands):
                other = oall_ref[m, :, lanes].astype(f32)
                kin[m] = kin[m] + jnp.sum(other * own, 0, keepdims=True)
                kin[bands + m] = kin[bands + m] + jnp.sum(
                    other[:grid_z] * own[grid_z:] - other[grid_z:] * own[:grid_z], 0, keepdims=True
                )
        lane = iota((1, LANES), 1)
        row = jnp.zeros((1, LANES), f32)
        for n in range(2 * bands):
            value = jnp.sum(sums[n], 0, keepdims=True) + kin[n]
            value = jnp.sum(value, 1, keepdims=True)
            for k, piece in enumerate(split3(value)):
                row = jnp.where(lane == 2 * bands * k + n, piece.astype(f32), row)
        sub = iota((16, LANES), 0)
        carried = jnp.where(sub == nch, jnp.broadcast_to(row, (16, LANES)), 0.0)
        out_ref[...] = (ret_ref[...] + carried[None]).astype(bf16)

    def finish(cm_ref, orb_ref, rr_ref, tab_ref, applied_ref, sub_ref):
        p = lax.axis_index("pw")
        radius = radius_rows(p, cm_ref, grid_x, grid_y, grid_z)
        got = rr_ref[...].astype(f32)
        right = jnp.concatenate(
            [got[:, h * 8 : (h + 1) * 8].reshape(count * 8, LANES) for h in range(2)], 1
        ).astype(bf16)
        z_back = dot(tab_ref[...], right)
        for h in range(2):
            lanes = slice(h * LANES, (h + 1) * LANES)
            values = orb_ref[:, lanes].astype(f32)
            result = kinetic_unit * radius[h].astype(f32) * values + z_back[:, lanes]
            applied_ref[:, lanes] = jnp.where(radius[h] <= KMAX * KMAX, result, 0.0)
        summed = jnp.sum(got[:, 0:8], 0)
        summed = summed + (
            pltpu.roll(summed, LANES - 2 * bands, 1) + pltpu.roll(summed, LANES - 4 * bands, 1)
        )
        summed = summed[nch : nch + 1] * (1.0 / (grid_z * count * 2 * LANES))
        sub_ref[0] = summed[:, 0:bands]
        sub_ref[1] = pltpu.roll(summed, LANES - bands, 1)[:, 0:bands]

    return to_columns, forward, backward, finish


class Late:
    def __init__(self, source, target, semaphore):
        self.copy = pltpu.make_async_copy(source, target, semaphore)
        self.target = target
        self.waiting = True
        self.copy.start()

    def __call__(self):
        if self.waiting:
            self.copy.wait()
            self.waiting = False
        return self.target


def call(kernel, out_shape, operands, scratch=(), late=(), mib=VMEM_MIB):
    vmem = pl.BlockSpec(memory_space=pltpu.VMEM)
    hbm = pl.BlockSpec(memory_space=pltpu.HBM)
    multiple = isinstance(out_shape, (list, tuple))
    n_in, n_out, n_own = len(operands), len(out_shape) if multiple else 1, len(scratch)

    def body(*refs):
        given, rest = list(refs[:n_in]), refs[n_in : n_in + n_out + n_own]
        if late:
            buffers, semaphores = refs[n_in + n_out + n_own : -1], refs[-1]
            for k, at in enumerate(late):
                given[at] = Late(given[at], buffers[k], semaphores.at[k])
        kernel(*given, *rest)

    extra = [pltpu.VMEM(operands[at].shape, operands[at].dtype) for at in late]
    if late:
        extra.append(pltpu.SemaphoreType.DMA((len(late),)))
    return pl.pallas_call(
        body,
        out_shape=out_shape,
        in_specs=[hbm if at in late else vmem for at in range(n_in)],
        out_specs=[vmem] * n_out if multiple else vmem,
        scratch_shapes=list(scratch) + extra,
        compiler_params=pltpu.CompilerParams(vmem_limit_bytes=mib * 1024 * 1024),
    )(*operands)


def per_device(orbitals, column_map, potential, projectors, block_index, block_atom, coupling):
    _, _, grid_z, col_local = orbitals.shape
    z_local, grid_x, grid_y = potential.shape
    natoms, nproj = coupling.shape[0], coupling.shape[1]
    entries = block_index.shape[0]
    count, bands = lax.axis_size("pw"), lax.axis_size("band")
    ncolumns = column_map.shape[0]
    half = box_half(grid_x, grid_y, ncolumns)
    zf, zb, yf, yft, xf, xb, yb, ybt = make_tables(grid_z, grid_x, grid_y, z_local, half)
    sizes = (grid_z, grid_x, grid_y, z_local, count, bands, natoms, nproj, entries, half)
    to_columns, forward, backward, finish = build(sizes)
    shape = jax.ShapeDtypeStruct
    blocks = z_local * grid_x * grid_y // BLOCK
    cj = 2 * nproj

    cm = column_map.reshape(ncolumns // LANES, LANES)
    orb = orbitals.reshape(2 * grid_z, col_local)
    bi = block_index.reshape(entries // LANES, LANES)
    at = block_atom.reshape(entries // LANES, LANES)
    coup = coupling.reshape(natoms, nproj * nproj).T
    proj = projectors.reshape(entries * nproj, BLOCK)
    packet = (count, 16, LANES)

    sent = call(to_columns, shape(packet, bf16), (cm, orb, zf), late=(0, 1, 2), mib=ALL_MIB)
    planes = lax.all_to_all(sent, "pw", split_axis=0, concat_axis=0, tiled=True)
    index_scratch = [pltpu.VMEM(cm.shape, i32), pltpu.VMEM(cm.shape, i32)]
    pf_scratch = pltpu.VMEM((entries * nproj, BLOCK), f32)
    real_space, window, to_send, near = call(
        forward,
        (shape((blocks, 2 * BLOCK), bf16), shape((cj, SLOTS), f32), shape((count, cj, LANES), f32),
         shape((nproj * nproj, SLOTS), f32)),
        (cm, planes, yf, yft, xf, bi, at, proj, coup),
        index_scratch + [pltpu.VMEM((2 * z_local * PACK, 256), f32), pf_scratch],
        late=(0, 2, 3, 4, 8, 5, 7, 6),
    )
    other = lax.all_to_all(to_send, "pw", split_axis=0, concat_axis=0, tiled=True)
    all_planes = lax.all_gather(planes, "band", axis=0, tiled=False)
    all_orb = lax.all_gather(orb, "band", axis=0, tiled=False)
    back = call(
        backward, shape(packet, bf16),
        (cm, other, window, real_space, potential, near, bi, at, proj, xb, yb, ybt, all_planes, all_orb),
        index_scratch
        + [pf_scratch, pltpu.VMEM((2 * z_local * PACK, 256), bf16), pltpu.VMEM(packet, f32)]
        + [pltpu.VMEM((z_local * grid_x, LANES), f32)] * 2,
        late=(7, 8, 6, 4, 9, 10, 11, 0, 12, 13),
    )
    returned = lax.all_to_all(back, "pw", split_axis=0, concat_axis=0, tiled=True)
    applied, sums = call(
        finish, (shape((2 * grid_z, col_local), f32), shape((2, 1, bands), f32)),
        (cm, orb, returned, zb),
    )
    applied = applied.reshape(1, 2, grid_z, col_local)
    return applied, sums.transpose(0, 2, 1)


def solution(mesh):
    in_specs = (
        P("band", None, None, "pw"),
        P(),
        P("pw", None, None),
        P("pw", None, None),
        P("pw"),
        P("pw"),
        P(),
    )
    out_specs = (P("band", None, None, "pw"), P(None, None, "band"))
    return jax.shard_map(
        per_device, mesh=mesh, in_specs=in_specs, out_specs=out_specs, check_vma=False
    )
```

```python
import math

import jax
import jax.numpy as jnp
import numpy as np
from jax import lax
from jax.experimental import pallas as pl
from jax.experimental.pallas import tpu as pltpu
from jax.sharding import PartitionSpec as P

KMAX = 73
BLOCK = 128
LANES = 128
VMEM_MIB, ALL_MIB = 52, 58
MAIN, TAIL = 80, 16
PACK = MAIN + TAIL
SLOTS = 256
kinetic_unit = 0.5 * (2.0 * math.pi / 58.6) ** 2
f32, bf16, i32 = jnp.float32, jnp.bfloat16, jnp.int32


def dft_table(length, sign):
    steps = np.arange(length, dtype=np.int32)
    product = steps[:, None] * steps[None, :] % length
    angles = product.astype(np.float32) * np.float32(2.0 * math.pi / length)
    root = np.float32(math.sqrt(length))
    cosines = np.cos(angles) / root
    sines = np.float32(sign) * np.sin(angles) / root
    return np.stack([np.stack([cosines, sines], 1), np.stack([-sines, cosines], 1)], 0).astype(np.float32)


def box_half(grid_x, grid_y, ncolumns):
    freq_x = np.arange(grid_x) - grid_x * (np.arange(grid_x) >= grid_x // 2)
    freq_y = np.arange(grid_y) - grid_y * (np.arange(grid_y) >= grid_y // 2)
    radius_sq = np.sort((freq_x[:, None] ** 2 + freq_y[None, :] ** 2).ravel())
    return int(math.isqrt(int(radius_sq[ncolumns - 1])))


def make_tables(grid_z, grid_x, grid_y, z_local, half):
    count = grid_z // z_local
    width = 2 * half + 1
    fwd_z, back_z = dft_table(grid_z, 1.0), dft_table(grid_z, -1.0)
    fwd_x, back_x = dft_table(grid_x, 1.0), dft_table(grid_x, -1.0)
    fwd_y, back_y = dft_table(grid_y, 1.0), dft_table(grid_y, -1.0)
    box_x = (np.arange(width) - half) % grid_x
    box_y = (np.arange(width) - half) % grid_y
    zf = np.zeros((count, 8, 2 * grid_z), np.float32)
    zb = np.zeros((2 * grid_z, count, 8), np.float32)
    for d in range(2):
        for plane in range(z_local):
            w = np.arange(count) * z_local + plane
            zf[:, d * z_local + plane, :] = fwd_z[:, :, d, w].reshape(2 * grid_z, count).T
            zb[:, :, d * z_local + plane] = back_z[d, w].reshape(count, 2 * grid_z).T
    split = LANES
    more = width - split
    pair = [np.arange(par, width, 2) for par in range(2)]
    beyond = [np.arange(split + par, width, 2) for par in range(2)]
    yf = np.zeros((2, split, 2, 256), np.float32)
    yf[:, :, :, :grid_y] = fwd_y[:, box_y[:split]]
    yft = np.zeros((2, 2, TAIL, 2, 256), np.float32)
    xf = np.zeros((2 * grid_x, 2, 2, MAIN), np.float32)
    xb = np.zeros((2, 2, MAIN, 2, grid_x), np.float32)
    order = np.concatenate([np.arange(0, grid_x, 2), np.arange(1, grid_x, 2)])
    yb = np.zeros((2, 256, 2, split), np.float32)
    yb[:, :grid_y] = back_y[:, :, :, box_y[:split]]
    ybt = np.zeros((2, 2, 2, TAIL, 256), np.float32)
    for par in range(2):
        xs, ys = box_x[pair[par]], box_y[beyond[par]]
        yft[:, par, : len(ys), :, :grid_y] = fwd_y[:, ys]
        for c in range(2):
            xf[:, c, par, : len(xs)] = fwd_x[c, xs][:, :, order].reshape(len(xs), 2 * grid_x).T
            for d in range(2):
                xb[d, par, : len(xs), c] = back_x[c, order][:, d, xs].T
                ybt[c, d, par, : len(ys), :grid_y] = back_y[c, :, d, ys]
    arrays = (
        zf.reshape(count * 8, -1), zb.reshape(2 * grid_z, -1), yf.reshape(2 * split, 512),
        yft.reshape(4 * TAIL, 512), xf.reshape(2 * grid_x, 4 * MAIN), xb.reshape(4 * MAIN, 2 * grid_x),
        yb.reshape(2, 256, 2 * split), ybt.reshape(2, 4 * TAIL, 256),
    )
    reach_x = math.isqrt((half + 1) ** 2 - 1 - (split - half) ** 2)
    assert (half + reach_x) // 2 < 64 and (more + 1) // 2 <= TAIL and half + 1 <= MAIN
    return [jnp.asarray(a.astype(jnp.bfloat16)) for a in arrays]


def dot(a, b, dims=((1,), (0,))):
    return lax.dot_general(a, b, (dims, ((), ())), preferred_element_type=f32)


def split3(x):
    hi = x.astype(bf16)
    rest = x - hi.astype(f32)
    mid = rest.astype(bf16)
    low = (rest - mid.astype(f32)).astype(bf16)
    return hi, mid, low


def iota(shape, axis):
    return lax.broadcasted_iota(i32, shape, axis)


def ones_where(mask):
    return jnp.where(mask, 1.0, 0.0).astype(bf16)


def quotient(values, divisor):
    return jnp.floor((values.astype(f32) + 0.5) * (1.0 / divisor)).astype(i32)


def frequencies(columns, grid_x, grid_y):
    x = quotient(columns, grid_y)
    y = columns - x * grid_y
    return jnp.where(x >= grid_x // 2, x - grid_x, x), jnp.where(y >= grid_y // 2, y - grid_y, y)


def radius_rows(p, cm_ref, grid_x, grid_y, grid_z):
    own = cm_ref[pl.ds(2 * p, 2), :]
    freq_x, freq_y = frequencies(own, grid_x, grid_y)
    flat = freq_x * freq_x + freq_y * freq_y
    row = iota((2 * grid_z, LANES), 0)
    z = jnp.where(row >= grid_z, row - grid_z, row)
    freq_z = jnp.where(z >= grid_z // 2, z - grid_z, z)
    sq = freq_z * freq_z
    return [sq + flat[h : h + 1, :] for h in range(2)]


def build(sizes):
    (grid_z, grid_x, grid_y, z_local, count, bands, natoms, nproj, entries, half) = sizes
    pairs = grid_x // 2
    blocks = z_local * grid_x * grid_y // BLOCK
    plane_blocks = blocks // z_local
    reach = natoms // count
    chunks = entries // LANES
    cj = 2 * nproj
    nch = 2 * z_local
    steps = 32
    gsteps = 32
    rows_c = z_local * PACK

    def block_rows(values):
        plane = quotient(values, plane_blocks)
        rest = values - plane * plane_blocks
        k = quotient(rest, 3)
        return plane * plane_blocks + (rest - 3 * k) * pairs + k

    def slots_of(values, p):
        start = p * natoms // count - 2 * reach
        t = values - start
        t = jnp.where(t < 0, t + natoms, t)
        return jnp.where(t >= natoms, t - natoms, t)

    def columns_of(rows):
        padded = jnp.concatenate([rows.astype(f32), jnp.zeros((8 - chunks, LANES), f32)], 0)
        return padded.T.astype(i32)

    def slot_onehot(at_ref, p):
        cols = columns_of(slots_of(at_ref[...], p))
        lane = iota((LANES, SLOTS), 1)
        return jnp.concatenate([ones_where(lane == cols[:, i : i + 1]) for i in range(chunks)], 0)

    def box_indices(cm_ref, row_ref, lane_ref):
        freq_x, freq_y = frequencies(cm_ref[...], grid_x, grid_y)
        x, y = freq_x + half, freq_y + half
        pair, parity, more = x >> 1, x & 1, y - LANES
        row_ref[...] = jnp.where(more >= 0, MAIN + (more >> 1), pair)
        lane_ref[...] = jnp.where(
            more >= 0, (more & 1) * LANES + parity * 64 + pair, parity * LANES + y
        )

    def near_coupling(p, coup):
        start = p * natoms // count - 2 * reach
        atom = start + iota((natoms, SLOTS), 1)
        atom = jnp.where(atom < 0, atom + natoms, atom)
        atom = jnp.where(atom >= natoms, atom - natoms, atom)
        select = ones_where(atom == iota((natoms, SLOTS), 0))
        near = dot(jnp.concatenate(split3(coup()[...]), 0), select)
        square = nproj * nproj
        return near[0:square] + near[square : 2 * square] + near[2 * square : 3 * square]

    def to_columns(cm, orb, table, out_ref):
        p = lax.axis_index("pw")
        radius = radius_rows(p, cm(), grid_x, grid_y, grid_z)
        orb_ref = orb()
        parts = []
        for h in range(2):
            values = orb_ref[:, h * LANES : (h + 1) * LANES].astype(f32)
            parts.append(jnp.where(radius[h] <= KMAX * KMAX, values, 0.0).astype(bf16))
        z = dot(table()[...], jnp.concatenate(parts, 1))
        out = [z[:, h * LANES : (h + 1) * LANES].reshape(count, 8, LANES) for h in range(2)]
        out_ref[...] = jnp.concatenate(out, 1).astype(bf16)

    def forward(cm, zr_ref, yf, yft, xf, bi, at, proj, coup,
                rs_ref, win_ref, send_ref, near_ref, xi_ref, yi_ref, acc_ref, pf_ref):
        p = lax.axis_index("pw")
        box_indices(cm(), xi_ref, yi_ref)
        acc_ref[...] = jnp.zeros_like(acc_ref)
        pack_row = iota((PACK, LANES), 0)
        pack_lane = iota((256, LANES), 0)

        def add_columns(step, carry):
            xrows = xi_ref[pl.ds(pl.multiple_of(step * 2 * steps, 8), 2 * steps), :]
            yrows = yi_ref[pl.ds(pl.multiple_of(step * 2 * steps, 8), 2 * steps), :]
            left, right = [], []
            for s in range(steps):
                v = zr_ref[step * steps + s].astype(f32)
                for h in range(2):
                    r = 2 * s + h
                    hot = ones_where(pack_row == xrows[r : r + 1, :]).reshape(PACK // 16, 16, LANES)
                    right.append(ones_where(pack_lane == yrows[r : r + 1, :]))
                    rows = []
                    for ch in range(nch):
                        one = v[h * 8 + ch : h * 8 + ch + 1, :]
                        wide = jnp.broadcast_to(one, (16, LANES)).astype(bf16)
                        rows.append((hot * wide[None]).reshape(PACK, LANES))
                    left.append(jnp.concatenate(rows, 0))
            acc_ref[...] += dot(jnp.concatenate(left, 1), jnp.concatenate(right, 1), ((1,), (1,)))
            return carry

        lax.fori_loop(0, count // steps, add_columns, 0)
        yf_ref, yft_ref, xf_ref = yf(), yft(), xf()
        main, tails = [], []
        for plane in range(z_local):
            starts = [c * rows_c + plane * PACK for c in range(2)]
            for par in range(2):
                lanes = slice(par * LANES, (par + 1) * LANES)
                main.append(jnp.concatenate([acc_ref[r : r + MAIN, lanes] for r in starts], 1))
            tails.append(
                jnp.concatenate(
                    [
                        acc_ref[r + MAIN : r + PACK, par * LANES : (par + 1) * LANES]
                        for r in starts
                        for par in range(2)
                    ],
                    0,
                ).astype(bf16)
            )
        ydone = dot(jnp.concatenate(main, 0).astype(bf16), yf_ref[...])
        lane = iota((pairs, LANES), 1)
        for plane in range(z_local):
            more = dot(tails[plane], yft_ref[...], ((0,), (0,)))
            mine = []
            for par in range(2):
                r = (plane * 2 + par) * MAIN
                mine.append(ydone[r : r + 64] + more[par * 64 : (par + 1) * 64])
                mine.append(ydone[r + 64 : r + MAIN])
            mine = jnp.concatenate(mine, 0).astype(bf16)
            real = dot(xf_ref[...], jnp.concatenate([mine[:, 0:256], mine[:, 256:512]], 0))
            for d in range(2):
                even = real[d * grid_x : d * grid_x + pairs]
                odd = real[d * grid_x + pairs : (d + 1) * grid_x]
                turned = pltpu.roll(odd[:, 0:128], 64, 1)
                middle = jnp.where(lane < 64, even[:, 128:256], turned)
                last = jnp.where(lane < 64, turned, pltpu.roll(odd[:, 128:256], 64, 1))
                for t, piece in enumerate((even[:, 0:128], middle, last)):
                    own = plane * plane_blocks + t * pairs
                    rs_ref[own : own + pairs, d * BLOCK : (d + 1) * BLOCK] = piece.astype(bf16)
        near_ref[...] = near_coupling(p, coup)
        pf_ref[...] = proj()[...].astype(f32)
        cols = columns_of(block_rows(bi()[...]))
        block_lane = iota((LANES, blocks), 1)
        hot = jnp.concatenate(
            [ones_where(block_lane == cols[:, i : i + 1]) for i in range(chunks)], 0
        )
        picked = dot(hot, rs_ref[...])
        select_row = iota((2 * BLOCK, LANES), 0)
        select_lane = iota((2 * BLOCK, LANES), 1)
        corr = jnp.zeros((entries, LANES), f32)
        for j in range(nproj):
            values = pf_ref[pl.ds(j, entries, stride=nproj), :]
            product = jnp.concatenate([values, values], 1) * picked
            hi = product.astype(bf16)
            low = (product - hi.astype(f32)).astype(bf16)
            target = jnp.where(select_row >= BLOCK, nproj + j, j)
            ones = ones_where(select_lane == target)
            corr = corr + (dot(hi, ones) + dot(low, ones))
        pieces = jnp.concatenate(split3(corr), 1)
        window = dot(pieces, slot_onehot(at(), p), ((0,), (0,)))
        window = window[0:cj] + window[LANES : LANES + cj] + window[2 * LANES : 2 * LANES + cj]
        win_ref[...] = window
        send_ref[...] = jnp.zeros_like(send_ref)
        home = p * natoms // count
        for s in range(1, 5):
            up = lax.rem(p + s, count)
            ahead = up * natoms // count - home
            ahead = jnp.where(ahead < 0, ahead + natoms, ahead)
            send_ref[up] = pltpu.roll(window, SLOTS - ahead, 1)[:, 0:LANES]
            down = lax.rem(p - s + count, count)
            send_ref[down] = window[:, 0:LANES]

    def backward(cm, xr_ref, win_ref, rs_ref, potential, near_ref, bi, at, proj,
                 xb, yb, ybt, zall, oall, out_ref,
                 xi_ref, yi_ref, pf_ref, grid_ref, ret_ref, pot_first, pot_rest):
        p = lax.axis_index("pw")
        home = p * natoms // count
        total = win_ref[...]
        nothing = jnp.zeros((cj, LANES), f32)
        for s in range(1, 5):
            down = lax.rem(p - s + count, count)
            total = total + jnp.concatenate([xr_ref[down], nothing], 1)
            up = lax.rem(p + s, count)
            ahead = up * natoms // count - home
            ahead = jnp.where(ahead < 0, ahead + natoms, ahead)
            total = total + pltpu.roll(jnp.concatenate([xr_ref[up], nothing], 1), ahead, 1)
        near = near_ref[...]
        near = near.reshape(nproj, nproj, SLOTS)
        weight = jnp.concatenate(
            [jnp.sum(near * total[c * nproj : (c + 1) * nproj][None], 1) for c in range(2)], 0
        ).astype(bf16)
        pf_ref[...] = proj()[...].astype(f32)
        ent_weight = dot(slot_onehot(at(), p), weight, ((1,), (1,)))
        terms = [jnp.zeros((entries, BLOCK), f32) for _ in range(2)]
        for j in range(nproj):
            values = pf_ref[pl.ds(j, entries, stride=nproj), :]
            for c in range(2):
                terms[c] = terms[c] + ent_weight[:, c * nproj + j : c * nproj + j + 1] * values
        pieces = jnp.concatenate(split3(jnp.concatenate(terms, 1)), 1)
        rows = block_rows(bi()[...])
        block_row = iota((blocks, LANES), 0)
        hot = jnp.concatenate(
            [ones_where(block_row == rows[i : i + 1, :]) for i in range(chunks)], 1
        )
        nonlocal_part = dot(hot, pieces)
        nonlocal_part = (
            nonlocal_part[:, 0:256] + nonlocal_part[:, 256:512] + nonlocal_part[:, 512:768]
        )
        pot_ref = potential()
        pot_first[...] = pot_ref[:, :, 0:LANES].reshape(z_local * grid_x, LANES)
        pot_rest[:, 0 : grid_y - LANES] = pot_ref[:, :, LANES:grid_y].reshape(
            z_local * grid_x, grid_y - LANES
        )
        xb_ref, yb_ref, ybt_ref = xb(), yb(), ybt()
        lane = iota((pairs, LANES), 1)
        backs = [[], []]
        for plane in range(z_local):
            first = plane * plane_blocks
            even, odd = (
                [
                    part[pl.ds(plane * grid_x + parity, pairs, stride=2), :]
                    for part in (pot_first, pot_rest)
                ]
                for parity in range(2)
            )
            turned = pltpu.roll(odd[0], 64, 1)
            pot = (
                even[0],
                jnp.where(lane < 64, even[1], turned),
                jnp.where(lane < 64, turned, pltpu.roll(odd[1], 64, 1)),
            )
            stacked = []
            for c in range(2):
                h = []
                for t in range(3):
                    own = slice(first + t * pairs, first + (t + 1) * pairs)
                    lanes = slice(c * BLOCK, (c + 1) * BLOCK)
                    h.append(pot[t] * rs_ref[own, lanes].astype(f32) + nonlocal_part[own, lanes])
                swung = pltpu.roll(h[2], 64, 1)
                stacked.append(jnp.concatenate([h[0], jnp.where(lane < 64, h[1], 0.0)], 1))
                stacked.append(
                    jnp.concatenate(
                        [
                            jnp.where(lane < 64, pltpu.roll(h[1], 64, 1), swung),
                            jnp.where(lane < 64, swung, 0.0),
                        ],
                        1,
                    )
                )
            x_back = dot(xb_ref[...], jnp.concatenate(stacked, 0).astype(bf16)).astype(bf16)
            tail = jnp.zeros((4 * TAIL, LANES), f32)
            for c in range(2):
                mine = x_back[c * 2 * MAIN : (c + 1) * 2 * MAIN]
                backs[c].append(mine)
                near_rows = jnp.concatenate([mine[0:64], mine[MAIN : MAIN + 64]], 0)
                tail = tail + dot(ybt_ref[c], near_rows, ((1,), (1,)))
            for d in range(2):
                for par in range(2):
                    r = d * rows_c + plane * PACK + MAIN
                    own = (2 * d + par) * TAIL
                    grid_ref[r : r + TAIL, par * LANES : (par + 1) * LANES] = tail[
                        own : own + TAIL
                    ].astype(bf16)
        y_back = dot(jnp.concatenate(backs[0], 0), yb_ref[0]) + dot(
            jnp.concatenate(backs[1], 0), yb_ref[1]
        )
        for plane in range(z_local):
            for par in range(2):
                own = (plane * 2 + par) * MAIN
                for d in range(2):
                    r = d * rows_c + plane * PACK
                    grid_ref[r : r + MAIN, par * LANES : (par + 1) * LANES] = y_back[
                        own : own + MAIN, d * LANES : (d + 1) * LANES
                    ].astype(bf16)
        cm_ref, zall_ref = cm(), zall()
        box_indices(cm_ref, xi_ref, yi_ref)
        pack_row = iota((PACK, LANES), 0)
        pack_lane = iota((256, LANES), 0)
        blank = jnp.zeros((8 - nch, LANES), f32)

        def take_columns(step, carry):
            base = pl.multiple_of(step * 2 * gsteps, 8)
            xrows = xi_ref[pl.ds(base, 2 * gsteps), :]
            yrows = yi_ref[pl.ds(base, 2 * gsteps), :]
            sums = list(carry)
            for s in range(gsteps):
                hot_y = jnp.concatenate(
                    [ones_where(pack_lane == yrows[2 * s + h : 2 * s + h + 1, :]) for h in range(2)], 1
                )
                taken = dot(grid_ref[...], hot_y)
                halves, swapped = [], []
                for h in range(2):
                    mask = ones_where(pack_row == xrows[2 * s + h : 2 * s + h + 1, :])
                    rows = []
                    for ch in range(nch):
                        part = taken[ch * PACK : (ch + 1) * PACK, h * LANES : (h + 1) * LANES]
                        part = (part.astype(bf16) * mask).reshape(PACK // 16, 16, LANES)
                        own = part[0]
                        for k in range(1, PACK // 16):
                            own = own + part[k]
                        rows.append(jnp.sum(own.astype(f32), 0, keepdims=True))
                    halves.append(jnp.concatenate(rows + [blank], 0))
                    other = rows[z_local:] + [-r for r in rows[:z_local]]
                    swapped.append(jnp.concatenate(other + [blank], 0))
                ret = jnp.concatenate(halves, 0)
                cross = jnp.concatenate(swapped, 0)
                ret_ref[step * gsteps + s] = ret
                for m in range(bands):
                    other = zall_ref[m, step * gsteps + s].astype(f32)
                    sums[m] = sums[m] + other * ret
                    sums[bands + m] = sums[bands + m] + other * cross
            return tuple(sums)

        zero = jnp.zeros((16, LANES), f32)
        sums = lax.fori_loop(0, count // gsteps, take_columns, (zero,) * (2 * bands))
        radius = radius_rows(p, cm_ref, grid_x, grid_y, grid_z)
        band = lax.axis_index("band")
        oall_ref = oall()
        kin = [jnp.zeros((1, LANES), f32) for _ in range(2 * bands)]
        for h in range(2):
            lanes = slice(h * LANES, (h + 1) * LANES)
            own = oall_ref[band, :, lanes].astype(f32)
            kinetic = jnp.where(radius[h] <= KMAX * KMAX, kinetic_unit * radius[h].astype(f32), 0.0)
            own = kinetic * own
            for m in range(bands):
                other = oall_ref[m, :, lanes].astype(f32)
                kin[m] = kin[m] + jnp.sum(other * own, 0, keepdims=True)
                kin[bands + m] = kin[bands + m] + jnp.sum(
                    other[:grid_z] * own[grid_z:] - other[grid_z:] * own[:grid_z], 0, keepdims=True
                )
        lane = iota((1, LANES), 1)
        row = jnp.zeros((1, LANES), f32)
        for n in range(2 * bands):
            value = jnp.sum(sums[n], 0, keepdims=True) + kin[n]
            value = jnp.sum(value, 1, keepdims=True)
            for k, piece in enumerate(split3(value)):
                row = jnp.where(lane == 2 * bands * k + n, piece.astype(f32), row)
        sub = iota((16, LANES), 0)
        carried = jnp.where(sub == nch, jnp.broadcast_to(row, (16, LANES)), 0.0)
        out_ref[...] = (ret_ref[...] + carried[None]).astype(bf16)

    def finish(cm_ref, orb_ref, rr_ref, tab_ref, applied_ref, sub_ref):
        p = lax.axis_index("pw")
        radius = radius_rows(p, cm_ref, grid_x, grid_y, grid_z)
        got = rr_ref[...].astype(f32)
        right = jnp.concatenate(
            [got[:, h * 8 : (h + 1) * 8].reshape(count * 8, LANES) for h in range(2)], 1
        ).astype(bf16)
        z_back = dot(tab_ref[...], right)
        for h in range(2):
            lanes = slice(h * LANES, (h + 1) * LANES)
            values = orb_ref[:, lanes].astype(f32)
            result = kinetic_unit * radius[h].astype(f32) * values + z_back[:, lanes]
            applied_ref[:, lanes] = jnp.where(radius[h] <= KMAX * KMAX, result, 0.0)
        summed = jnp.sum(got[:, 0:8], 0)
        summed = summed + (
            pltpu.roll(summed, LANES - 2 * bands, 1) + pltpu.roll(summed, LANES - 4 * bands, 1)
        )
        summed = summed[nch : nch + 1] * (1.0 / (grid_z * count * 2 * LANES))
        sub_ref[0] = summed[:, 0:bands]
        sub_ref[1] = pltpu.roll(summed, LANES - bands, 1)[:, 0:bands]

    return to_columns, forward, backward, finish


class Late:
    def __init__(self, source, target, semaphore):
        self.copy = pltpu.make_async_copy(source, target, semaphore)
        self.target = target
        self.waiting = True
        self.copy.start()

    def __call__(self):
        if self.waiting:
            self.copy.wait()
            self.waiting = False
        return self.target


def call(kernel, out_shape, operands, scratch=(), late=(), mib=VMEM_MIB):
    vmem = pl.BlockSpec(memory_space=pltpu.VMEM)
    hbm = pl.BlockSpec(memory_space=pltpu.HBM)
    multiple = isinstance(out_shape, (list, tuple))
    n_in, n_out, n_own = len(operands), len(out_shape) if multiple else 1, len(scratch)

    def body(*refs):
        given, rest = list(refs[:n_in]), refs[n_in : n_in + n_out + n_own]
        if late:
            buffers, semaphores = refs[n_in + n_out + n_own : -1], refs[-1]
            for k, at in enumerate(late):
                given[at] = Late(given[at], buffers[k], semaphores.at[k])
        kernel(*given, *rest)

    extra = [pltpu.VMEM(operands[at].shape, operands[at].dtype) for at in late]
    if late:
        extra.append(pltpu.SemaphoreType.DMA((len(late),)))
    return pl.pallas_call(
        body,
        out_shape=out_shape,
        in_specs=[hbm if at in late else vmem for at in range(n_in)],
        out_specs=[vmem] * n_out if multiple else vmem,
        scratch_shapes=list(scratch) + extra,
        compiler_params=pltpu.CompilerParams(vmem_limit_bytes=mib * 1024 * 1024),
    )(*operands)


def per_device(orbitals, column_map, potential, projectors, block_index, block_atom, coupling):
    _, _, grid_z, col_local = orbitals.shape
    z_local, grid_x, grid_y = potential.shape
    natoms, nproj = coupling.shape[0], coupling.shape[1]
    entries = block_index.shape[0]
    count, bands = lax.axis_size("pw"), lax.axis_size("band")
    ncolumns = column_map.shape[0]
    half = box_half(grid_x, grid_y, ncolumns)
    zf, zb, yf, yft, xf, xb, yb, ybt = make_tables(grid_z, grid_x, grid_y, z_local, half)
    sizes = (grid_z, grid_x, grid_y, z_local, count, bands, natoms, nproj, entries, half)
    to_columns, forward, backward, finish = build(sizes)
    shape = jax.ShapeDtypeStruct
    blocks = z_local * grid_x * grid_y // BLOCK
    cj = 2 * nproj

    cm = column_map.reshape(ncolumns // LANES, LANES)
    orb = orbitals.reshape(2 * grid_z, col_local)
    bi = block_index.reshape(entries // LANES, LANES)
    at = block_atom.reshape(entries // LANES, LANES)
    coup = coupling.reshape(natoms, nproj * nproj).T
    proj = projectors.reshape(entries * nproj, BLOCK)
    packet = (count, 16, LANES)

    sent = call(to_columns, shape(packet, bf16), (cm, orb, zf), late=(0, 1, 2), mib=ALL_MIB)
    planes = lax.all_to_all(sent, "pw", split_axis=0, concat_axis=0, tiled=True)
    index_scratch = [pltpu.VMEM(cm.shape, i32), pltpu.VMEM(cm.shape, i32)]
    pf_scratch = pltpu.VMEM((entries * nproj, BLOCK), f32)
    real_space, window, to_send, near = call(
        forward,
        (shape((blocks, 2 * BLOCK), bf16), shape((cj, SLOTS), f32), shape((count, cj, LANES), f32),
         shape((nproj * nproj, SLOTS), f32)),
        (cm, planes, yf, yft, xf, bi, at, proj, coup),
        index_scratch + [pltpu.VMEM((2 * z_local * PACK, 256), f32), pf_scratch],
        late=(0, 2, 3, 4, 8, 5, 7, 6),
    )
    other = lax.all_to_all(to_send, "pw", split_axis=0, concat_axis=0, tiled=True)
    all_planes = lax.all_gather(planes, "band", axis=0, tiled=False)
    all_orb = lax.all_gather(orb, "band", axis=0, tiled=False)
    back = call(
        backward, shape(packet, bf16),
        (cm, other, window, real_space, potential, near, bi, at, proj, xb, yb, ybt, all_planes, all_orb),
        index_scratch
        + [pf_scratch, pltpu.VMEM((2 * z_local * PACK, 256), bf16), pltpu.VMEM(packet, f32)]
        + [pltpu.VMEM((z_local * grid_x, LANES), f32)] * 2,
        late=(7, 8, 6, 4, 9, 10, 11, 0, 12, 13), mib=50,
    )
    returned = lax.all_to_all(back, "pw", split_axis=0, concat_axis=0, tiled=True)
    applied, sums = call(
        finish, (shape((2 * grid_z, col_local), f32), shape((2, 1, bands), f32)),
        (cm, orb, returned, zb),
    )
    applied = applied.reshape(1, 2, grid_z, col_local)
    return applied, sums.transpose(0, 2, 1)


def solution(mesh):
    in_specs = (
        P("band", None, None, "pw"),
        P(),
        P("pw", None, None),
        P("pw", None, None),
        P("pw"),
        P("pw"),
        P(),
    )
    out_specs = (P("band", None, None, "pw"), P(None, None, "band"))
    return jax.shard_map(
        per_device, mesh=mesh, in_specs=in_specs, out_specs=out_specs, check_vma=False
    )
```

```python
import math

import jax
import jax.numpy as jnp
import numpy as np
from jax import lax
from jax.experimental import pallas as pl
from jax.experimental.pallas import tpu as pltpu
from jax.sharding import PartitionSpec as P

KMAX = 73
BLOCK = 128
LANES = 128
VMEM_MIB, ALL_MIB = 52, 58
MAIN, TAIL = 80, 16
PACK = MAIN + TAIL
SLOTS = 256
kinetic_unit = 0.5 * (2.0 * math.pi / 58.6) ** 2
f32, bf16, i32 = jnp.float32, jnp.bfloat16, jnp.int32


def dft_table(length, sign):
    steps = np.arange(length, dtype=np.int32)
    product = steps[:, None] * steps[None, :] % length
    angles = product.astype(np.float32) * np.float32(2.0 * math.pi / length)
    root = np.float32(math.sqrt(length))
    cosines = np.cos(angles) / root
    sines = np.float32(sign) * np.sin(angles) / root
    return np.stack([np.stack([cosines, sines], 1), np.stack([-sines, cosines], 1)], 0).astype(np.float32)


def box_half(grid_x, grid_y, ncolumns):
    freq_x = np.arange(grid_x) - grid_x * (np.arange(grid_x) >= grid_x // 2)
    freq_y = np.arange(grid_y) - grid_y * (np.arange(grid_y) >= grid_y // 2)
    radius_sq = np.sort((freq_x[:, None] ** 2 + freq_y[None, :] ** 2).ravel())
    return int(math.isqrt(int(radius_sq[ncolumns - 1])))


def make_tables(grid_z, grid_x, grid_y, z_local, half):
    count = grid_z // z_local
    width = 2 * half + 1
    fwd_z, back_z = dft_table(grid_z, 1.0), dft_table(grid_z, -1.0)
    fwd_x, back_x = dft_table(grid_x, 1.0), dft_table(grid_x, -1.0)
    fwd_y, back_y = dft_table(grid_y, 1.0), dft_table(grid_y, -1.0)
    box_x = (np.arange(width) - half) % grid_x
    box_y = (np.arange(width) - half) % grid_y
    zf = np.zeros((count, 8, 2 * grid_z), np.float32)
    zb = np.zeros((2 * grid_z, count, 8), np.float32)
    for d in range(2):
        for plane in range(z_local):
            w = np.arange(count) * z_local + plane
            zf[:, d * z_local + plane, :] = fwd_z[:, :, d, w].reshape(2 * grid_z, count).T
            zb[:, :, d * z_local + plane] = back_z[d, w].reshape(count, 2 * grid_z).T
    split = LANES
    more = width - split
    pair = [np.arange(par, width, 2) for par in range(2)]
    beyond = [np.arange(split + par, width, 2) for par in range(2)]
    yf = np.zeros((2, split, 2, 256), np.float32)
    yf[:, :, :, :grid_y] = fwd_y[:, box_y[:split]]
    yft = np.zeros((2, 2, TAIL, 2, 256), np.float32)
    xf = np.zeros((2 * grid_x, 2, 2, MAIN), np.float32)
    xb = np.zeros((2, 2, MAIN, 2, grid_x), np.float32)
    order = np.concatenate([np.arange(0, grid_x, 2), np.arange(1, grid_x, 2)])
    yb = np.zeros((2, 256, 2, split), np.float32)
    yb[:, :grid_y] = back_y[:, :, :, box_y[:split]]
    ybt = np.zeros((2, 2, 2, TAIL, 256), np.float32)
    for par in range(2):
        xs, ys = box_x[pair[par]], box_y[beyond[par]]
        yft[:, par, : len(ys), :, :grid_y] = fwd_y[:, ys]
        for c in range(2):
            xf[:, c, par, : len(xs)] = fwd_x[c, xs][:, :, order].reshape(len(xs), 2 * grid_x).T
            for d in range(2):
                xb[d, par, : len(xs), c] = back_x[c, order][:, d, xs].T
                ybt[c, d, par, : len(ys), :grid_y] = back_y[c, :, d, ys]
    arrays = (
        zf.reshape(count * 8, -1), zb.reshape(2 * grid_z, -1), yf.reshape(2 * split, 512),
        yft.reshape(4 * TAIL, 512), xf.reshape(2 * grid_x, 4 * MAIN), xb.reshape(4 * MAIN, 2 * grid_x),
        yb.reshape(2, 256, 2 * split), ybt.reshape(2, 4 * TAIL, 256),
    )
    reach_x = math.isqrt((half + 1) ** 2 - 1 - (split - half) ** 2)
    assert (half + reach_x) // 2 < 64 and (more + 1) // 2 <= TAIL and half + 1 <= MAIN
    return [jnp.asarray(a.astype(jnp.bfloat16)) for a in arrays]


def dot(a, b, dims=((1,), (0,))):
    return lax.dot_general(a, b, (dims, ((), ())), preferred_element_type=f32)


def split3(x):
    hi = x.astype(bf16)
    rest = x - hi.astype(f32)
    mid = rest.astype(bf16)
    low = (rest - mid.astype(f32)).astype(bf16)
    return hi, mid, low


def iota(shape, axis):
    return lax.broadcasted_iota(i32, shape, axis)


def ones_where(mask):
    return jnp.where(mask, 1.0, 0.0).astype(bf16)


def quotient(values, divisor):
    return jnp.floor((values.astype(f32) + 0.5) * (1.0 / divisor)).astype(i32)


def frequencies(columns, grid_x, grid_y):
    x = quotient(columns, grid_y)
    y = columns - x * grid_y
    return jnp.where(x >= grid_x // 2, x - grid_x, x), jnp.where(y >= grid_y // 2, y - grid_y, y)


def radius_rows(p, cm_ref, grid_x, grid_y, grid_z):
    own = cm_ref[pl.ds(2 * p, 2), :]
    freq_x, freq_y = frequencies(own, grid_x, grid_y)
    flat = freq_x * freq_x + freq_y * freq_y
    row = iota((2 * grid_z, LANES), 0)
    z = jnp.where(row >= grid_z, row - grid_z, row)
    freq_z = jnp.where(z >= grid_z // 2, z - grid_z, z)
    sq = freq_z * freq_z
    return [sq + flat[h : h + 1, :] for h in range(2)]


def build(sizes):
    (grid_z, grid_x, grid_y, z_local, count, bands, natoms, nproj, entries, half) = sizes
    pairs = grid_x // 2
    blocks = z_local * grid_x * grid_y // BLOCK
    plane_blocks = blocks // z_local
    reach = natoms // count
    chunks = entries // LANES
    cj = 2 * nproj
    nch = 2 * z_local
    steps = 32
    gsteps = 32
    rows_c = z_local * PACK

    def block_rows(values):
        plane = quotient(values, plane_blocks)
        rest = values - plane * plane_blocks
        k = quotient(rest, 3)
        return plane * plane_blocks + (rest - 3 * k) * pairs + k

    def slots_of(values, p):
        start = p * natoms // count - 2 * reach
        t = values - start
        t = jnp.where(t < 0, t + natoms, t)
        return jnp.where(t >= natoms, t - natoms, t)

    def columns_of(rows):
        padded = jnp.concatenate([rows.astype(f32), jnp.zeros((8 - chunks, LANES), f32)], 0)
        return padded.T.astype(i32)

    def slot_onehot(at_ref, p):
        cols = columns_of(slots_of(at_ref[...], p))
        lane = iota((LANES, SLOTS), 1)
        return jnp.concatenate([ones_where(lane == cols[:, i : i + 1]) for i in range(chunks)], 0)

    def box_indices(cm_ref, row_ref, lane_ref):
        freq_x, freq_y = frequencies(cm_ref[...], grid_x, grid_y)
        x, y = freq_x + half, freq_y + half
        pair, parity, more = x >> 1, x & 1, y - LANES
        row_ref[...] = jnp.where(more >= 0, MAIN + (more >> 1), pair)
        lane_ref[...] = jnp.where(
            more >= 0, (more & 1) * LANES + parity * 64 + pair, parity * LANES + y
        )

    def near_coupling(p, coup):
        start = p * natoms // count - 2 * reach
        atom = start + iota((natoms, SLOTS), 1)
        atom = jnp.where(atom < 0, atom + natoms, atom)
        atom = jnp.where(atom >= natoms, atom - natoms, atom)
        select = ones_where(atom == iota((natoms, SLOTS), 0))
        near = dot(jnp.concatenate(split3(coup()[...]), 0), select)
        square = nproj * nproj
        return near[0:square] + near[square : 2 * square] + near[2 * square : 3 * square]

    def hot_rows(numbers, row, count):
        wide = jnp.broadcast_to(row.astype(f32), (16, LANES)).astype(bf16)
        same = numbers.reshape(count // 16, 16, LANES) == wide[None]
        return jnp.where(same, jnp.ones((), bf16), jnp.zeros((), bf16))

    def to_columns(cm, orb, table, out_ref):
        p = lax.axis_index("pw")
        radius = radius_rows(p, cm(), grid_x, grid_y, grid_z)
        orb_ref = orb()
        parts = []
        for h in range(2):
            values = orb_ref[:, h * LANES : (h + 1) * LANES].astype(f32)
            parts.append(jnp.where(radius[h] <= KMAX * KMAX, values, 0.0).astype(bf16))
        z = dot(table()[...], jnp.concatenate(parts, 1))
        out = [z[:, h * LANES : (h + 1) * LANES].reshape(count, 8, LANES) for h in range(2)]
        out_ref[...] = jnp.concatenate(out, 1).astype(bf16)

    def forward(cm, zr_ref, yf, yft, xf, bi, at, proj, coup,
                rs_ref, win_ref, send_ref, near_ref, xi_ref, yi_ref, acc_ref, pf_ref):
        p = lax.axis_index("pw")
        box_indices(cm(), xi_ref, yi_ref)
        acc_ref[...] = jnp.zeros_like(acc_ref)
        pack_row = iota((PACK, LANES), 0).astype(f32).astype(bf16)
        pack_lane = iota((256, LANES), 0).astype(f32).astype(bf16)

        def add_columns(step, carry):
            xrows = xi_ref[pl.ds(pl.multiple_of(step * 2 * steps, 8), 2 * steps), :]
            yrows = yi_ref[pl.ds(pl.multiple_of(step * 2 * steps, 8), 2 * steps), :]
            left, right = [], []
            for s in range(steps):
                v = zr_ref[step * steps + s].astype(f32)
                for h in range(2):
                    r = 2 * s + h
                    hot = hot_rows(pack_row, xrows[r : r + 1, :], PACK)
                    right.append(hot_rows(pack_lane, yrows[r : r + 1, :], 256).reshape(256, LANES))
                    rows = []
                    for ch in range(nch):
                        one = v[h * 8 + ch : h * 8 + ch + 1, :]
                        wide = jnp.broadcast_to(one, (16, LANES)).astype(bf16)
                        rows.append((hot * wide[None]).reshape(PACK, LANES))
                    left.append(jnp.concatenate(rows, 0))
            acc_ref[...] += dot(jnp.concatenate(left, 1), jnp.concatenate(right, 1), ((1,), (1,)))
            return carry

        lax.fori_loop(0, count // steps, add_columns, 0)
        yf_ref, yft_ref, xf_ref = yf(), yft(), xf()
        main, tails = [], []
        for plane in range(z_local):
            starts = [c * rows_c + plane * PACK for c in range(2)]
            for par in range(2):
                lanes = slice(par * LANES, (par + 1) * LANES)
                main.append(jnp.concatenate([acc_ref[r : r + MAIN, lanes] for r in starts], 1))
            tails.append(
                jnp.concatenate(
                    [
                        acc_ref[r + MAIN : r + PACK, par * LANES : (par + 1) * LANES]
                        for r in starts
                        for par in range(2)
                    ],
                    0,
                ).astype(bf16)
            )
        ydone = dot(jnp.concatenate(main, 0).astype(bf16), yf_ref[...])
        lane = iota((pairs, LANES), 1)
        for plane in range(z_local):
            more = dot(tails[plane], yft_ref[...], ((0,), (0,)))
            mine = []
            for par in range(2):
                r = (plane * 2 + par) * MAIN
                mine.append(ydone[r : r + 64] + more[par * 64 : (par + 1) * 64])
                mine.append(ydone[r + 64 : r + MAIN])
            mine = jnp.concatenate(mine, 0).astype(bf16)
            real = dot(xf_ref[...], jnp.concatenate([mine[:, 0:256], mine[:, 256:512]], 0))
            for d in range(2):
                even = real[d * grid_x : d * grid_x + pairs]
                odd = real[d * grid_x + pairs : (d + 1) * grid_x]
                turned = pltpu.roll(odd[:, 0:128], 64, 1)
                middle = jnp.where(lane < 64, even[:, 128:256], turned)
                last = jnp.where(lane < 64, turned, pltpu.roll(odd[:, 128:256], 64, 1))
                for t, piece in enumerate((even[:, 0:128], middle, last)):
                    own = plane * plane_blocks + t * pairs
                    rs_ref[own : own + pairs, d * BLOCK : (d + 1) * BLOCK] = piece.astype(bf16)
        near_ref[...] = near_coupling(p, coup)
        pf_ref[...] = proj()[...].astype(f32)
        cols = columns_of(block_rows(bi()[...]))
        block_lane = iota((LANES, blocks), 1)
        hot = jnp.concatenate(
            [ones_where(block_lane == cols[:, i : i + 1]) for i in range(chunks)], 0
        )
        picked = dot(hot, rs_ref[...])
        select_row = iota((2 * BLOCK, LANES), 0)
        select_lane = iota((2 * BLOCK, LANES), 1)
        corr = jnp.zeros((entries, LANES), f32)
        for j in range(nproj):
            values = pf_ref[pl.ds(j, entries, stride=nproj), :]
            product = jnp.concatenate([values, values], 1) * picked
            hi = product.astype(bf16)
            low = (product - hi.astype(f32)).astype(bf16)
            target = jnp.where(select_row >= BLOCK, nproj + j, j)
            ones = ones_where(select_lane == target)
            corr = corr + (dot(hi, ones) + dot(low, ones))
        pieces = jnp.concatenate(split3(corr), 1)
        window = dot(pieces, slot_onehot(at(), p), ((0,), (0,)))
        window = window[0:cj] + window[LANES : LANES + cj] + window[2 * LANES : 2 * LANES + cj]
        win_ref[...] = window
        send_ref[...] = jnp.zeros_like(send_ref)
        home = p * natoms // count
        for s in range(1, 5):
            up = lax.rem(p + s, count)
            ahead = up * natoms // count - home
            ahead = jnp.where(ahead < 0, ahead + natoms, ahead)
            send_ref[up] = pltpu.roll(window, SLOTS - ahead, 1)[:, 0:LANES]
            down = lax.rem(p - s + count, count)
            send_ref[down] = window[:, 0:LANES]

    def backward(cm, xr_ref, win_ref, rs_ref, potential, near_ref, bi, at, proj,
                 xb, yb, ybt, zall, oall, out_ref,
                 xi_ref, yi_ref, pf_ref, grid_ref, ret_ref, pot_first, pot_rest):
        p = lax.axis_index("pw")
        home = p * natoms // count
        total = win_ref[...]
        nothing = jnp.zeros((cj, LANES), f32)
        for s in range(1, 5):
            down = lax.rem(p - s + count, count)
            total = total + jnp.concatenate([xr_ref[down], nothing], 1)
            up = lax.rem(p + s, count)
            ahead = up * natoms // count - home
            ahead = jnp.where(ahead < 0, ahead + natoms, ahead)
            total = total + pltpu.roll(jnp.concatenate([xr_ref[up], nothing], 1), ahead, 1)
        near = near_ref[...]
        near = near.reshape(nproj, nproj, SLOTS)
        weight = jnp.concatenate(
            [jnp.sum(near * total[c * nproj : (c + 1) * nproj][None], 1) for c in range(2)], 0
        ).astype(bf16)
        pf_ref[...] = proj()[...].astype(f32)
        ent_weight = dot(slot_onehot(at(), p), weight, ((1,), (1,)))
        terms = [jnp.zeros((entries, BLOCK), f32) for _ in range(2)]
        for j in range(nproj):
            values = pf_ref[pl.ds(j, entries, stride=nproj), :]
            for c in range(2):
                terms[c] = terms[c] + ent_weight[:, c * nproj + j : c * nproj + j + 1] * values
        pieces = jnp.concatenate(split3(jnp.concatenate(terms, 1)), 1)
        rows = block_rows(bi()[...])
        block_row = iota((blocks, LANES), 0)
        hot = jnp.concatenate(
            [ones_where(block_row == rows[i : i + 1, :]) for i in range(chunks)], 1
        )
        nonlocal_part = dot(hot, pieces)
        nonlocal_part = (
            nonlocal_part[:, 0:256] + nonlocal_part[:, 256:512] + nonlocal_part[:, 512:768]
        )
        pot_ref = potential()
        pot_first[...] = pot_ref[:, :, 0:LANES].reshape(z_local * grid_x, LANES)
        pot_rest[:, 0 : grid_y - LANES] = pot_ref[:, :, LANES:grid_y].reshape(
            z_local * grid_x, grid_y - LANES
        )
        xb_ref, yb_ref, ybt_ref = xb(), yb(), ybt()
        lane = iota((pairs, LANES), 1)
        backs = [[], []]
        for plane in range(z_local):
            first = plane * plane_blocks
            even, odd = (
                [
                    part[pl.ds(plane * grid_x + parity, pairs, stride=2), :]
                    for part in (pot_first, pot_rest)
                ]
                for parity in range(2)
            )
            turned = pltpu.roll(odd[0], 64, 1)
            pot = (
                even[0],
                jnp.where(lane < 64, even[1], turned),
                jnp.where(lane < 64, turned, pltpu.roll(odd[1], 64, 1)),
            )
            stacked = []
            for c in range(2):
                h = []
                for t in range(3):
                    own = slice(first + t * pairs, first + (t + 1) * pairs)
                    lanes = slice(c * BLOCK, (c + 1) * BLOCK)
                    h.append(pot[t] * rs_ref[own, lanes].astype(f32) + nonlocal_part[own, lanes])
                swung = pltpu.roll(h[2], 64, 1)
                stacked.append(jnp.concatenate([h[0], jnp.where(lane < 64, h[1], 0.0)], 1))
                stacked.append(
                    jnp.concatenate(
                        [
                            jnp.where(lane < 64, pltpu.roll(h[1], 64, 1), swung),
                            jnp.where(lane < 64, swung, 0.0),
                        ],
                        1,
                    )
                )
            x_back = dot(xb_ref[...], jnp.concatenate(stacked, 0).astype(bf16)).astype(bf16)
            tail = jnp.zeros((4 * TAIL, LANES), f32)
            for c in range(2):
                mine = x_back[c * 2 * MAIN : (c + 1) * 2 * MAIN]
                backs[c].append(mine)
                near_rows = jnp.concatenate([mine[0:64], mine[MAIN : MAIN + 64]], 0)
                tail = tail + dot(ybt_ref[c], near_rows, ((1,), (1,)))
            for d in range(2):
                for par in range(2):
                    r = d * rows_c + plane * PACK + MAIN
                    own = (2 * d + par) * TAIL
                    grid_ref[r : r + TAIL, par * LANES : (par + 1) * LANES] = tail[
                        own : own + TAIL
                    ].astype(bf16)
        y_back = dot(jnp.concatenate(backs[0], 0), yb_ref[0]) + dot(
            jnp.concatenate(backs[1], 0), yb_ref[1]
        )
        for plane in range(z_local):
            for par in range(2):
                own = (plane * 2 + par) * MAIN
                for d in range(2):
                    r = d * rows_c + plane * PACK
                    grid_ref[r : r + MAIN, par * LANES : (par + 1) * LANES] = y_back[
                        own : own + MAIN, d * LANES : (d + 1) * LANES
                    ].astype(bf16)
        cm_ref, zall_ref = cm(), zall()
        box_indices(cm_ref, xi_ref, yi_ref)
        pack_row = iota((PACK, LANES), 0).astype(f32).astype(bf16)
        pack_lane = iota((256, LANES), 0).astype(f32).astype(bf16)
        blank = jnp.zeros((8 - nch, LANES), f32)

        def take_columns(step, carry):
            base = pl.multiple_of(step * 2 * gsteps, 8)
            xrows = xi_ref[pl.ds(base, 2 * gsteps), :]
            yrows = yi_ref[pl.ds(base, 2 * gsteps), :]
            sums = list(carry)
            for s in range(gsteps):
                hot_y = jnp.concatenate(
                    [hot_rows(pack_lane, yrows[2 * s + h : 2 * s + h + 1, :], 256).reshape(256, LANES) for h in range(2)], 1
                )
                taken = dot(grid_ref[...], hot_y)
                halves, swapped = [], []
                for h in range(2):
                    mask = hot_rows(pack_row, xrows[2 * s + h : 2 * s + h + 1, :], PACK).reshape(PACK, LANES)
                    rows = []
                    for ch in range(nch):
                        part = taken[ch * PACK : (ch + 1) * PACK, h * LANES : (h + 1) * LANES]
                        part = (part.astype(bf16) * mask).reshape(PACK // 16, 16, LANES)
                        own = part[0]
                        for k in range(1, PACK // 16):
                            own = own + part[k]
                        rows.append(jnp.sum(own.astype(f32), 0, keepdims=True))
                    halves.append(jnp.concatenate(rows + [blank], 0))
                    other = rows[z_local:] + [-r for r in rows[:z_local]]
                    swapped.append(jnp.concatenate(other + [blank], 0))
                ret = jnp.concatenate(halves, 0)
                cross = jnp.concatenate(swapped, 0)
                ret_ref[step * gsteps + s] = ret
                for m in range(bands):
                    other = zall_ref[m, step * gsteps + s].astype(f32)
                    sums[m] = sums[m] + other * ret
                    sums[bands + m] = sums[bands + m] + other * cross
            return tuple(sums)

        zero = jnp.zeros((16, LANES), f32)
        sums = lax.fori_loop(0, count // gsteps, take_columns, (zero,) * (2 * bands))
        radius = radius_rows(p, cm_ref, grid_x, grid_y, grid_z)
        band = lax.axis_index("band")
        oall_ref = oall()
        kin = [jnp.zeros((1, LANES), f32) for _ in range(2 * bands)]
        for h in range(2):
            lanes = slice(h * LANES, (h + 1) * LANES)
            own = oall_ref[band, :, lanes].astype(f32)
            kinetic = jnp.where(radius[h] <= KMAX * KMAX, kinetic_unit * radius[h].astype(f32), 0.0)
            own = kinetic * own
            for m in range(bands):
                other = oall_ref[m, :, lanes].astype(f32)
                kin[m] = kin[m] + jnp.sum(other * own, 0, keepdims=True)
                kin[bands + m] = kin[bands + m] + jnp.sum(
                    other[:grid_z] * own[grid_z:] - other[grid_z:] * own[:grid_z], 0, keepdims=True
                )
        lane = iota((1, LANES), 1)
        row = jnp.zeros((1, LANES), f32)
        for n in range(2 * bands):
            value = jnp.sum(sums[n], 0, keepdims=True) + kin[n]
            value = jnp.sum(value, 1, keepdims=True)
            for k, piece in enumerate(split3(value)):
                row = jnp.where(lane == 2 * bands * k + n, piece.astype(f32), row)
        sub = iota((16, LANES), 0)
        carried = jnp.where(sub == nch, jnp.broadcast_to(row, (16, LANES)), 0.0)
        out_ref[...] = (ret_ref[...] + carried[None]).astype(bf16)

    def finish(cm_ref, orb_ref, rr_ref, tab_ref, applied_ref, sub_ref):
        p = lax.axis_index("pw")
        radius = radius_rows(p, cm_ref, grid_x, grid_y, grid_z)
        got = rr_ref[...].astype(f32)
        right = jnp.concatenate(
            [got[:, h * 8 : (h + 1) * 8].reshape(count * 8, LANES) for h in range(2)], 1
        ).astype(bf16)
        z_back = dot(tab_ref[...], right)
        for h in range(2):
            lanes = slice(h * LANES, (h + 1) * LANES)
            values = orb_ref[:, lanes].astype(f32)
            result = kinetic_unit * radius[h].astype(f32) * values + z_back[:, lanes]
            applied_ref[:, lanes] = jnp.where(radius[h] <= KMAX * KMAX, result, 0.0)
        summed = jnp.sum(got[:, 0:8], 0)
        summed = summed + (
            pltpu.roll(summed, LANES - 2 * bands, 1) + pltpu.roll(summed, LANES - 4 * bands, 1)
        )
        summed = summed[nch : nch + 1] * (1.0 / (grid_z * count * 2 * LANES))
        sub_ref[0] = summed[:, 0:bands]
        sub_ref[1] = pltpu.roll(summed, LANES - bands, 1)[:, 0:bands]

    return to_columns, forward, backward, finish


class Late:
    def __init__(self, source, target, semaphore):
        self.copy = pltpu.make_async_copy(source, target, semaphore)
        self.target = target
        self.waiting = True
        self.copy.start()

    def __call__(self):
        if self.waiting:
            self.copy.wait()
            self.waiting = False
        return self.target


def call(kernel, out_shape, operands, scratch=(), late=(), mib=VMEM_MIB):
    vmem = pl.BlockSpec(memory_space=pltpu.VMEM)
    hbm = pl.BlockSpec(memory_space=pltpu.HBM)
    multiple = isinstance(out_shape, (list, tuple))
    n_in, n_out, n_own = len(operands), len(out_shape) if multiple else 1, len(scratch)

    def body(*refs):
        given, rest = list(refs[:n_in]), refs[n_in : n_in + n_out + n_own]
        if late:
            buffers, semaphores = refs[n_in + n_out + n_own : -1], refs[-1]
            for k, at in enumerate(late):
                given[at] = Late(given[at], buffers[k], semaphores.at[k])
        kernel(*given, *rest)

    extra = [pltpu.VMEM(operands[at].shape, operands[at].dtype) for at in late]
    if late:
        extra.append(pltpu.SemaphoreType.DMA((len(late),)))
    return pl.pallas_call(
        body,
        out_shape=out_shape,
        in_specs=[hbm if at in late else vmem for at in range(n_in)],
        out_specs=[vmem] * n_out if multiple else vmem,
        scratch_shapes=list(scratch) + extra,
        compiler_params=pltpu.CompilerParams(vmem_limit_bytes=mib * 1024 * 1024),
    )(*operands)


def per_device(orbitals, column_map, potential, projectors, block_index, block_atom, coupling):
    _, _, grid_z, col_local = orbitals.shape
    z_local, grid_x, grid_y = potential.shape
    natoms, nproj = coupling.shape[0], coupling.shape[1]
    entries = block_index.shape[0]
    count, bands = lax.axis_size("pw"), lax.axis_size("band")
    ncolumns = column_map.shape[0]
    half = box_half(grid_x, grid_y, ncolumns)
    zf, zb, yf, yft, xf, xb, yb, ybt = make_tables(grid_z, grid_x, grid_y, z_local, half)
    sizes = (grid_z, grid_x, grid_y, z_local, count, bands, natoms, nproj, entries, half)
    to_columns, forward, backward, finish = build(sizes)
    shape = jax.ShapeDtypeStruct
    blocks = z_local * grid_x * grid_y // BLOCK
    cj = 2 * nproj

    cm = column_map.reshape(ncolumns // LANES, LANES)
    orb = orbitals.reshape(2 * grid_z, col_local)
    bi = block_index.reshape(entries // LANES, LANES)
    at = block_atom.reshape(entries // LANES, LANES)
    coup = coupling.reshape(natoms, nproj * nproj).T
    proj = projectors.reshape(entries * nproj, BLOCK)
    packet = (count, 16, LANES)

    sent = call(to_columns, shape(packet, bf16), (cm, orb, zf), late=(0, 1, 2), mib=ALL_MIB)
    planes = lax.all_to_all(sent, "pw", split_axis=0, concat_axis=0, tiled=True)
    index_scratch = [pltpu.VMEM(cm.shape, i32), pltpu.VMEM(cm.shape, i32)]
    pf_scratch = pltpu.VMEM((entries * nproj, BLOCK), f32)
    real_space, window, to_send, near = call(
        forward,
        (shape((blocks, 2 * BLOCK), bf16), shape((cj, SLOTS), f32), shape((count, cj, LANES), f32),
         shape((nproj * nproj, SLOTS), f32)),
        (cm, planes, yf, yft, xf, bi, at, proj, coup),
        index_scratch + [pltpu.VMEM((2 * z_local * PACK, 256), f32), pf_scratch],
        late=(0, 2, 3, 4, 8, 5, 7, 6),
    )
    other = lax.all_to_all(to_send, "pw", split_axis=0, concat_axis=0, tiled=True)
    all_planes = lax.all_gather(planes, "band", axis=0, tiled=False)
    all_orb = lax.all_gather(orb, "band", axis=0, tiled=False)
    back = call(
        backward, shape(packet, bf16),
        (cm, other, window, real_space, potential, near, bi, at, proj, xb, yb, ybt, all_planes, all_orb),
        index_scratch
        + [pf_scratch, pltpu.VMEM((2 * z_local * PACK, 256), bf16), pltpu.VMEM(packet, f32)]
        + [pltpu.VMEM((z_local * grid_x, LANES), f32)] * 2,
        late=(7, 8, 6, 4, 9, 10, 11, 0, 12, 13), mib=50,
    )
    returned = lax.all_to_all(back, "pw", split_axis=0, concat_axis=0, tiled=True)
    applied, sums = call(
        finish, (shape((2 * grid_z, col_local), f32), shape((2, 1, bands), f32)),
        (cm, orb, returned, zb),
    )
    applied = applied.reshape(1, 2, grid_z, col_local)
    return applied, sums.transpose(0, 2, 1)


def solution(mesh):
    in_specs = (
        P("band", None, None, "pw"),
        P(),
        P("pw", None, None),
        P("pw", None, None),
        P("pw"),
        P("pw"),
        P(),
    )
    out_specs = (P("band", None, None, "pw"), P(None, None, "band"))
    return jax.shard_map(
        per_device, mesh=mesh, in_specs=in_specs, out_specs=out_specs, check_vma=False
    )
```

```python
import math

import jax
import jax.numpy as jnp
import numpy as np
from jax import lax
from jax.experimental import pallas as pl
from jax.experimental.pallas import tpu as pltpu
from jax.sharding import PartitionSpec as P

KMAX = 73
BLOCK = 128
LANES = 128
VMEM_MIB, ALL_MIB = 52, 58
MAIN, TAIL = 80, 16
PACK = MAIN + TAIL
SLOTS = 256
kinetic_unit = 0.5 * (2.0 * math.pi / 58.6) ** 2
f32, bf16, i32 = jnp.float32, jnp.bfloat16, jnp.int32


def dft_table(length, sign):
    steps = np.arange(length, dtype=np.int32)
    product = steps[:, None] * steps[None, :] % length
    angles = product.astype(np.float32) * np.float32(2.0 * math.pi / length)
    root = np.float32(math.sqrt(length))
    cosines = np.cos(angles) / root
    sines = np.float32(sign) * np.sin(angles) / root
    return np.stack([np.stack([cosines, sines], 1), np.stack([-sines, cosines], 1)], 0).astype(np.float32)


def box_half(grid_x, grid_y, ncolumns):
    freq_x = np.arange(grid_x) - grid_x * (np.arange(grid_x) >= grid_x // 2)
    freq_y = np.arange(grid_y) - grid_y * (np.arange(grid_y) >= grid_y // 2)
    radius_sq = np.sort((freq_x[:, None] ** 2 + freq_y[None, :] ** 2).ravel())
    return int(math.isqrt(int(radius_sq[ncolumns - 1])))


def make_tables(grid_z, grid_x, grid_y, z_local, half):
    count = grid_z // z_local
    width = 2 * half + 1
    fwd_z, back_z = dft_table(grid_z, 1.0), dft_table(grid_z, -1.0)
    fwd_x, back_x = dft_table(grid_x, 1.0), dft_table(grid_x, -1.0)
    fwd_y, back_y = dft_table(grid_y, 1.0), dft_table(grid_y, -1.0)
    box_x = (np.arange(width) - half) % grid_x
    box_y = (np.arange(width) - half) % grid_y
    zf = np.zeros((count, 8, 2 * grid_z), np.float32)
    zb = np.zeros((2 * grid_z, count, 8), np.float32)
    for d in range(2):
        for plane in range(z_local):
            w = np.arange(count) * z_local + plane
            zf[:, d * z_local + plane, :] = fwd_z[:, :, d, w].reshape(2 * grid_z, count).T
            zb[:, :, d * z_local + plane] = back_z[d, w].reshape(count, 2 * grid_z).T
    split = LANES
    more = width - split
    pair = [np.arange(par, width, 2) for par in range(2)]
    beyond = [np.arange(split + par, width, 2) for par in range(2)]
    yf = np.zeros((2, split, 2, 256), np.float32)
    yf[:, :, :, :grid_y] = fwd_y[:, box_y[:split]]
    yft = np.zeros((2, 2, TAIL, 2, 256), np.float32)
    xf = np.zeros((2 * grid_x, 2, 2, MAIN), np.float32)
    xb = np.zeros((2, 2, MAIN, 2, grid_x), np.float32)
    order = np.concatenate([np.arange(0, grid_x, 2), np.arange(1, grid_x, 2)])
    yb = np.zeros((2, 256, 2, split), np.float32)
    yb[:, :grid_y] = back_y[:, :, :, box_y[:split]]
    ybt = np.zeros((2, 2, 2, TAIL, 256), np.float32)
    for par in range(2):
        xs, ys = box_x[pair[par]], box_y[beyond[par]]
        yft[:, par, : len(ys), :, :grid_y] = fwd_y[:, ys]
        for c in range(2):
            xf[:, c, par, : len(xs)] = fwd_x[c, xs][:, :, order].reshape(len(xs), 2 * grid_x).T
            for d in range(2):
                xb[d, par, : len(xs), c] = back_x[c, order][:, d, xs].T
                ybt[c, d, par, : len(ys), :grid_y] = back_y[c, :, d, ys]
    arrays = (
        zf.reshape(count * 8, -1), zb.reshape(2 * grid_z, -1), yf.reshape(2 * split, 512),
        yft.reshape(4 * TAIL, 512), xf.reshape(2 * grid_x, 4 * MAIN), xb.reshape(4 * MAIN, 2 * grid_x),
        yb.reshape(2, 256, 2 * split), ybt.reshape(2, 4 * TAIL, 256),
    )
    reach_x = math.isqrt((half + 1) ** 2 - 1 - (split - half) ** 2)
    assert (half + reach_x) // 2 < 64 and (more + 1) // 2 <= TAIL and half + 1 <= MAIN
    return [jnp.asarray(a.astype(jnp.bfloat16)) for a in arrays]


def dot(a, b, dims=((1,), (0,))):
    return lax.dot_general(a, b, (dims, ((), ())), preferred_element_type=f32)


def split3(x):
    hi = x.astype(bf16)
    rest = x - hi.astype(f32)
    mid = rest.astype(bf16)
    low = (rest - mid.astype(f32)).astype(bf16)
    return hi, mid, low


def iota(shape, axis):
    return lax.broadcasted_iota(i32, shape, axis)


def ones_where(mask):
    return jnp.where(mask, 1.0, 0.0).astype(bf16)


def quotient(values, divisor):
    return jnp.floor((values.astype(f32) + 0.5) * (1.0 / divisor)).astype(i32)


def frequencies(columns, grid_x, grid_y):
    x = quotient(columns, grid_y)
    y = columns - x * grid_y
    return jnp.where(x >= grid_x // 2, x - grid_x, x), jnp.where(y >= grid_y // 2, y - grid_y, y)


def radius_rows(p, cm_ref, grid_x, grid_y, grid_z):
    own = cm_ref[pl.ds(2 * p, 2), :]
    freq_x, freq_y = frequencies(own, grid_x, grid_y)
    flat = freq_x * freq_x + freq_y * freq_y
    row = iota((2 * grid_z, LANES), 0)
    z = jnp.where(row >= grid_z, row - grid_z, row)
    freq_z = jnp.where(z >= grid_z // 2, z - grid_z, z)
    sq = freq_z * freq_z
    return [sq + flat[h : h + 1, :] for h in range(2)]


def build(sizes):
    (grid_z, grid_x, grid_y, z_local, count, bands, natoms, nproj, entries, half) = sizes
    pairs = grid_x // 2
    blocks = z_local * grid_x * grid_y // BLOCK
    plane_blocks = blocks // z_local
    reach = natoms // count
    chunks = entries // LANES
    cj = 2 * nproj
    nch = 2 * z_local
    steps = 32
    gsteps = 32
    rows_c = z_local * PACK

    def block_rows(values):
        plane = quotient(values, plane_blocks)
        rest = values - plane * plane_blocks
        k = quotient(rest, 3)
        return plane * plane_blocks + (rest - 3 * k) * pairs + k

    def slots_of(values, p):
        start = p * natoms // count - 2 * reach
        t = values - start
        t = jnp.where(t < 0, t + natoms, t)
        return jnp.where(t >= natoms, t - natoms, t)

    def columns_of(rows):
        padded = jnp.concatenate([rows.astype(f32), jnp.zeros((8 - chunks, LANES), f32)], 0)
        return padded.T.astype(i32)

    def slot_onehot(at_ref, p):
        cols = columns_of(slots_of(at_ref[...], p))
        lane = iota((LANES, SLOTS), 1)
        return jnp.concatenate([ones_where(lane == cols[:, i : i + 1]) for i in range(chunks)], 0)

    def box_indices(cm_ref, row_ref, lane_ref):
        freq_x, freq_y = frequencies(cm_ref[...], grid_x, grid_y)
        x, y = freq_x + half, freq_y + half
        pair, parity, more = x >> 1, x & 1, y - LANES
        row_ref[...] = jnp.where(more >= 0, MAIN + (more >> 1), pair)
        lane_ref[...] = jnp.where(
            more >= 0, (more & 1) * LANES + parity * 64 + pair, parity * LANES + y
        )

    def near_coupling(p, coup):
        start = p * natoms // count - 2 * reach
        atom = start + iota((natoms, SLOTS), 1)
        atom = jnp.where(atom < 0, atom + natoms, atom)
        atom = jnp.where(atom >= natoms, atom - natoms, atom)
        select = ones_where(atom == iota((natoms, SLOTS), 0))
        near = dot(jnp.concatenate(split3(coup()[...]), 0), select)
        square = nproj * nproj
        return near[0:square] + near[square : 2 * square] + near[2 * square : 3 * square]

    def hot_rows(numbers, row, count):
        wide = jnp.broadcast_to(row.astype(f32), (16, LANES)).astype(bf16)
        same = numbers.reshape(count // 16, 16, LANES) == wide[None]
        return jnp.where(same, jnp.ones((), bf16), jnp.zeros((), bf16))

    def to_columns(cm, orb, table, out_ref):
        p = lax.axis_index("pw")
        radius = radius_rows(p, cm(), grid_x, grid_y, grid_z)
        orb_ref = orb()
        parts = []
        for h in range(2):
            values = orb_ref[:, h * LANES : (h + 1) * LANES].astype(f32)
            parts.append(jnp.where(radius[h] <= KMAX * KMAX, values, 0.0).astype(bf16))
        z = dot(table()[...], jnp.concatenate(parts, 1))
        out = [z[:, h * LANES : (h + 1) * LANES].reshape(count, 8, LANES) for h in range(2)]
        out_ref[...] = jnp.concatenate(out, 1).astype(bf16)

    def forward(cm, zr_ref, yf, yft, xf, bi, at, proj, coup,
                rs_ref, win_ref, send_ref, near_ref, xi_ref, yi_ref, acc_ref, pf_ref):
        p = lax.axis_index("pw")
        box_indices(cm(), xi_ref, yi_ref)
        acc_ref[...] = jnp.zeros_like(acc_ref)
        pack_row = iota((PACK, LANES), 0).astype(f32).astype(bf16)
        pack_lane = iota((256, LANES), 0).astype(f32).astype(bf16)

        def add_columns(step, carry):
            xrows = xi_ref[pl.ds(pl.multiple_of(step * 2 * steps, 8), 2 * steps), :]
            yrows = yi_ref[pl.ds(pl.multiple_of(step * 2 * steps, 8), 2 * steps), :]
            left, right = [], []
            for s in range(steps):
                v = zr_ref[step * steps + s].astype(f32)
                for h in range(2):
                    r = 2 * s + h
                    hot = hot_rows(pack_row, xrows[r : r + 1, :], PACK)
                    right.append(hot_rows(pack_lane, yrows[r : r + 1, :], 256).reshape(256, LANES))
                    rows = []
                    for ch in range(nch):
                        one = v[h * 8 + ch : h * 8 + ch + 1, :]
                        wide = jnp.broadcast_to(one, (16, LANES)).astype(bf16)
                        rows.append((hot * wide[None]).reshape(PACK, LANES))
                    left.append(jnp.concatenate(rows, 0))
            acc_ref[...] += dot(jnp.concatenate(left, 1), jnp.concatenate(right, 1), ((1,), (1,)))
            return carry

        lax.fori_loop(0, count // steps, add_columns, 0)
        yf_ref, yft_ref, xf_ref = yf(), yft(), xf()
        main, tails = [], []
        for plane in range(z_local):
            starts = [c * rows_c + plane * PACK for c in range(2)]
            for par in range(2):
                lanes = slice(par * LANES, (par + 1) * LANES)
                main.append(jnp.concatenate([acc_ref[r : r + MAIN, lanes] for r in starts], 1))
            tails.append(
                jnp.concatenate(
                    [
                        acc_ref[r + MAIN : r + PACK, par * LANES : (par + 1) * LANES]
                        for r in starts
                        for par in range(2)
                    ],
                    0,
                ).astype(bf16)
            )
        ydone = dot(jnp.concatenate(main, 0).astype(bf16), yf_ref[...])
        lane = iota((pairs, LANES), 1)
        for plane in range(z_local):
            more = dot(tails[plane], yft_ref[...], ((0,), (0,)))
            mine = []
            for par in range(2):
                r = (plane * 2 + par) * MAIN
                mine.append(ydone[r : r + 64] + more[par * 64 : (par + 1) * 64])
                mine.append(ydone[r + 64 : r + MAIN])
            mine = jnp.concatenate(mine, 0).astype(bf16)
            real = dot(xf_ref[...], jnp.concatenate([mine[:, 0:256], mine[:, 256:512]], 0))
            for d in range(2):
                even = real[d * grid_x : d * grid_x + pairs]
                odd = real[d * grid_x + pairs : (d + 1) * grid_x]
                turned = pltpu.roll(odd[:, 0:128], 64, 1)
                middle = jnp.where(lane < 64, even[:, 128:256], turned)
                last = jnp.where(lane < 64, turned, pltpu.roll(odd[:, 128:256], 64, 1))
                for t, piece in enumerate((even[:, 0:128], middle, last)):
                    own = plane * plane_blocks + t * pairs
                    rs_ref[own : own + pairs, d * BLOCK : (d + 1) * BLOCK] = piece.astype(bf16)
        near_ref[...] = near_coupling(p, coup)
        pf_ref[...] = proj()[...].astype(f32)
        cols = columns_of(block_rows(bi()[...]))
        block_lane = iota((LANES, blocks), 1)
        hot = jnp.concatenate(
            [ones_where(block_lane == cols[:, i : i + 1]) for i in range(chunks)], 0
        )
        picked = dot(hot, rs_ref[...])
        select_row = iota((2 * BLOCK, LANES), 0)
        select_lane = iota((2 * BLOCK, LANES), 1)
        corr = jnp.zeros((entries, LANES), f32)
        for j in range(nproj):
            values = pf_ref[pl.ds(j, entries, stride=nproj), :]
            product = jnp.concatenate([values, values], 1) * picked
            hi = product.astype(bf16)
            low = (product - hi.astype(f32)).astype(bf16)
            target = jnp.where(select_row >= BLOCK, nproj + j, j)
            ones = ones_where(select_lane == target)
            corr = corr + (dot(hi, ones) + dot(low, ones))
        pieces = jnp.concatenate(split3(corr), 1)
        window = dot(pieces, slot_onehot(at(), p), ((0,), (0,)))
        window = window[0:cj] + window[LANES : LANES + cj] + window[2 * LANES : 2 * LANES + cj]
        win_ref[...] = window
        send_ref[...] = jnp.zeros_like(send_ref)
        home = p * natoms // count
        for s in range(1, 5):
            up = lax.rem(p + s, count)
            ahead = up * natoms // count - home
            ahead = jnp.where(ahead < 0, ahead + natoms, ahead)
            send_ref[up] = pltpu.roll(window, SLOTS - ahead, 1)[:, 0:LANES]
            down = lax.rem(p - s + count, count)
            send_ref[down] = window[:, 0:LANES]

    def backward(cm, xr_ref, win_ref, rs_ref, potential, near_ref, bi, at, proj,
                 xb, yb, ybt, zall, oall, out_ref,
                 xi_ref, yi_ref, pf_ref, grid_ref, ret_ref, pot_first, pot_rest):
        p = lax.axis_index("pw")
        home = p * natoms // count
        total = win_ref[...]
        nothing = jnp.zeros((cj, LANES), f32)
        for s in range(1, 5):
            down = lax.rem(p - s + count, count)
            total = total + jnp.concatenate([xr_ref[down], nothing], 1)
            up = lax.rem(p + s, count)
            ahead = up * natoms // count - home
            ahead = jnp.where(ahead < 0, ahead + natoms, ahead)
            total = total + pltpu.roll(jnp.concatenate([xr_ref[up], nothing], 1), ahead, 1)
        near = near_ref[...]
        near = near.reshape(nproj, nproj, SLOTS)
        weight = jnp.concatenate(
            [jnp.sum(near * total[c * nproj : (c + 1) * nproj][None], 1) for c in range(2)], 0
        ).astype(bf16)
        pf_ref[...] = proj()[...].astype(f32)
        ent_weight = dot(slot_onehot(at(), p), weight, ((1,), (1,)))
        ent_weight = ent_weight.astype(bf16)
        spread_row = iota((cj, 2 * BLOCK), 0)
        spread_part = jnp.where(iota((cj, 2 * BLOCK), 1) >= BLOCK, nproj, 0)
        terms = jnp.zeros((entries, 2 * BLOCK), f32)
        for j in range(nproj):
            values = pf_ref[pl.ds(j, entries, stride=nproj), :]
            wide = dot(ent_weight, ones_where(spread_row == spread_part + j))
            terms = terms + wide * jnp.concatenate([values, values], 1)
        pieces = jnp.concatenate(split3(terms), 1)
        rows = block_rows(bi()[...])
        block_row = iota((blocks, LANES), 0)
        hot = jnp.concatenate(
            [ones_where(block_row == rows[i : i + 1, :]) for i in range(chunks)], 1
        )
        nonlocal_part = dot(hot, pieces)
        nonlocal_part = (
            nonlocal_part[:, 0:256] + nonlocal_part[:, 256:512] + nonlocal_part[:, 512:768]
        )
        pot_ref = potential()
        pot_first[...] = pot_ref[:, :, 0:LANES].reshape(z_local * grid_x, LANES)
        pot_rest[:, 0 : grid_y - LANES] = pot_ref[:, :, LANES:grid_y].reshape(
            z_local * grid_x, grid_y - LANES
        )
        xb_ref, yb_ref, ybt_ref = xb(), yb(), ybt()
        lane = iota((pairs, LANES), 1)
        backs = [[], []]
        for plane in range(z_local):
            first = plane * plane_blocks
            even, odd = (
                [
                    part[pl.ds(plane * grid_x + parity, pairs, stride=2), :]
                    for part in (pot_first, pot_rest)
                ]
                for parity in range(2)
            )
            turned = pltpu.roll(odd[0], 64, 1)
            pot = (
                even[0],
                jnp.where(lane < 64, even[1], turned),
                jnp.where(lane < 64, turned, pltpu.roll(odd[1], 64, 1)),
            )
            stacked = []
            for c in range(2):
                h = []
                for t in range(3):
                    own = slice(first + t * pairs, first + (t + 1) * pairs)
                    lanes = slice(c * BLOCK, (c + 1) * BLOCK)
                    h.append(pot[t] * rs_ref[own, lanes].astype(f32) + nonlocal_part[own, lanes])
                swung = pltpu.roll(h[2], 64, 1)
                stacked.append(jnp.concatenate([h[0], jnp.where(lane < 64, h[1], 0.0)], 1))
                stacked.append(
                    jnp.concatenate(
                        [
                            jnp.where(lane < 64, pltpu.roll(h[1], 64, 1), swung),
                            jnp.where(lane < 64, swung, 0.0),
                        ],
                        1,
                    )
                )
            x_back = dot(xb_ref[...], jnp.concatenate(stacked, 0).astype(bf16)).astype(bf16)
            tail = jnp.zeros((4 * TAIL, LANES), f32)
            for c in range(2):
                mine = x_back[c * 2 * MAIN : (c + 1) * 2 * MAIN]
                backs[c].append(mine)
                near_rows = jnp.concatenate([mine[0:64], mine[MAIN : MAIN + 64]], 0)
                tail = tail + dot(ybt_ref[c], near_rows, ((1,), (1,)))
            for d in range(2):
                for par in range(2):
                    r = d * rows_c + plane * PACK + MAIN
                    own = (2 * d + par) * TAIL
                    grid_ref[r : r + TAIL, par * LANES : (par + 1) * LANES] = tail[
                        own : own + TAIL
                    ].astype(bf16)
        y_back = dot(jnp.concatenate(backs[0], 0), yb_ref[0]) + dot(
            jnp.concatenate(backs[1], 0), yb_ref[1]
        )
        for plane in range(z_local):
            for par in range(2):
                own = (plane * 2 + par) * MAIN
                for d in range(2):
                    r = d * rows_c + plane * PACK
                    grid_ref[r : r + MAIN, par * LANES : (par + 1) * LANES] = y_back[
                        own : own + MAIN, d * LANES : (d + 1) * LANES
                    ].astype(bf16)
        cm_ref, zall_ref = cm(), zall()
        box_indices(cm_ref, xi_ref, yi_ref)
        pack_row = iota((PACK, LANES), 0).astype(f32).astype(bf16)
        pack_lane = iota((256, LANES), 0).astype(f32).astype(bf16)
        blank = jnp.zeros((8 - nch, LANES), f32)

        def take_columns(step, carry):
            base = pl.multiple_of(step * 2 * gsteps, 8)
            xrows = xi_ref[pl.ds(base, 2 * gsteps), :]
            yrows = yi_ref[pl.ds(base, 2 * gsteps), :]
            sums = list(carry)
            for s in range(gsteps):
                hot_y = jnp.concatenate(
                    [hot_rows(pack_lane, yrows[2 * s + h : 2 * s + h + 1, :], 256).reshape(256, LANES) for h in range(2)], 1
                )
                taken = dot(grid_ref[...], hot_y)
                halves, swapped = [], []
                for h in range(2):
                    mask = hot_rows(pack_row, xrows[2 * s + h : 2 * s + h + 1, :], PACK).reshape(PACK, LANES)
                    rows = []
                    for ch in range(nch):
                        part = taken[ch * PACK : (ch + 1) * PACK, h * LANES : (h + 1) * LANES]
                        part = (part.astype(bf16) * mask).reshape(PACK // 16, 16, LANES)
                        own = part[0]
                        for k in range(1, PACK // 16):
                            own = own + part[k]
                        rows.append(jnp.sum(own.astype(f32), 0, keepdims=True))
                    halves.append(jnp.concatenate(rows + [blank], 0))
                    other = rows[z_local:] + [-r for r in rows[:z_local]]
                    swapped.append(jnp.concatenate(other + [blank], 0))
                ret = jnp.concatenate(halves, 0)
                cross = jnp.concatenate(swapped, 0)
                ret_ref[step * gsteps + s] = ret
                for m in range(bands):
                    other = zall_ref[m, step * gsteps + s].astype(f32)
                    sums[m] = sums[m] + other * ret
                    sums[bands + m] = sums[bands + m] + other * cross
            return tuple(sums)

        zero = jnp.zeros((16, LANES), f32)
        sums = lax.fori_loop(0, count // gsteps, take_columns, (zero,) * (2 * bands))
        radius = radius_rows(p, cm_ref, grid_x, grid_y, grid_z)
        band = lax.axis_index("band")
        oall_ref = oall()
        kin = [jnp.zeros((1, LANES), f32) for _ in range(2 * bands)]
        for h in range(2):
            lanes = slice(h * LANES, (h + 1) * LANES)
            own = oall_ref[band, :, lanes].astype(f32)
            kinetic = jnp.where(radius[h] <= KMAX * KMAX, kinetic_unit * radius[h].astype(f32), 0.0)
            own = kinetic * own
            for m in range(bands):
                other = oall_ref[m, :, lanes].astype(f32)
                kin[m] = kin[m] + jnp.sum(other * own, 0, keepdims=True)
                kin[bands + m] = kin[bands + m] + jnp.sum(
                    other[:grid_z] * own[grid_z:] - other[grid_z:] * own[:grid_z], 0, keepdims=True
                )
        lane = iota((1, LANES), 1)
        row = jnp.zeros((1, LANES), f32)
        for n in range(2 * bands):
            value = jnp.sum(sums[n], 0, keepdims=True) + kin[n]
            value = jnp.sum(value, 1, keepdims=True)
            for k, piece in enumerate(split3(value)):
                row = jnp.where(lane == 2 * bands * k + n, piece.astype(f32), row)
        sub = iota((16, LANES), 0)
        carried = jnp.where(sub == nch, jnp.broadcast_to(row, (16, LANES)), 0.0)
        out_ref[...] = (ret_ref[...] + carried[None]).astype(bf16)

    def finish(cm_ref, orb_ref, rr_ref, tab_ref, applied_ref, sub_ref):
        p = lax.axis_index("pw")
        radius = radius_rows(p, cm_ref, grid_x, grid_y, grid_z)
        got = rr_ref[...].astype(f32)
        right = jnp.concatenate(
            [got[:, h * 8 : (h + 1) * 8].reshape(count * 8, LANES) for h in range(2)], 1
        ).astype(bf16)
        z_back = dot(tab_ref[...], right)
        for h in range(2):
            lanes = slice(h * LANES, (h + 1) * LANES)
            values = orb_ref[:, lanes].astype(f32)
            result = kinetic_unit * radius[h].astype(f32) * values + z_back[:, lanes]
            applied_ref[:, lanes] = jnp.where(radius[h] <= KMAX * KMAX, result, 0.0)
        summed = jnp.sum(got[:, 0:8], 0)
        summed = summed + (
            pltpu.roll(summed, LANES - 2 * bands, 1) + pltpu.roll(summed, LANES - 4 * bands, 1)
        )
        summed = summed[nch : nch + 1] * (1.0 / (grid_z * count * 2 * LANES))
        sub_ref[0] = summed[:, 0:bands]
        sub_ref[1] = pltpu.roll(summed, LANES - bands, 1)[:, 0:bands]

    return to_columns, forward, backward, finish


class Late:
    def __init__(self, source, target, semaphore):
        self.copy = pltpu.make_async_copy(source, target, semaphore)
        self.target = target
        self.waiting = True
        self.copy.start()

    def __call__(self):
        if self.waiting:
            self.copy.wait()
            self.waiting = False
        return self.target


def call(kernel, out_shape, operands, scratch=(), late=(), mib=VMEM_MIB):
    vmem = pl.BlockSpec(memory_space=pltpu.VMEM)
    hbm = pl.BlockSpec(memory_space=pltpu.HBM)
    multiple = isinstance(out_shape, (list, tuple))
    n_in, n_out, n_own = len(operands), len(out_shape) if multiple else 1, len(scratch)

    def body(*refs):
        given, rest = list(refs[:n_in]), refs[n_in : n_in + n_out + n_own]
        if late:
            buffers, semaphores = refs[n_in + n_out + n_own : -1], refs[-1]
            for k, at in enumerate(late):
                given[at] = Late(given[at], buffers[k], semaphores.at[k])
        kernel(*given, *rest)

    extra = [pltpu.VMEM(operands[at].shape, operands[at].dtype) for at in late]
    if late:
        extra.append(pltpu.SemaphoreType.DMA((len(late),)))
    return pl.pallas_call(
        body,
        out_shape=out_shape,
        in_specs=[hbm if at in late else vmem for at in range(n_in)],
        out_specs=[vmem] * n_out if multiple else vmem,
        scratch_shapes=list(scratch) + extra,
        compiler_params=pltpu.CompilerParams(vmem_limit_bytes=mib * 1024 * 1024),
    )(*operands)


def per_device(orbitals, column_map, potential, projectors, block_index, block_atom, coupling):
    _, _, grid_z, col_local = orbitals.shape
    z_local, grid_x, grid_y = potential.shape
    natoms, nproj = coupling.shape[0], coupling.shape[1]
    entries = block_index.shape[0]
    count, bands = lax.axis_size("pw"), lax.axis_size("band")
    ncolumns = column_map.shape[0]
    half = box_half(grid_x, grid_y, ncolumns)
    zf, zb, yf, yft, xf, xb, yb, ybt = make_tables(grid_z, grid_x, grid_y, z_local, half)
    sizes = (grid_z, grid_x, grid_y, z_local, count, bands, natoms, nproj, entries, half)
    to_columns, forward, backward, finish = build(sizes)
    shape = jax.ShapeDtypeStruct
    blocks = z_local * grid_x * grid_y // BLOCK
    cj = 2 * nproj

    cm = column_map.reshape(ncolumns // LANES, LANES)
    orb = orbitals.reshape(2 * grid_z, col_local)
    bi = block_index.reshape(entries // LANES, LANES)
    at = block_atom.reshape(entries // LANES, LANES)
    coup = coupling.reshape(natoms, nproj * nproj).T
    proj = projectors.reshape(entries * nproj, BLOCK)
    packet = (count, 16, LANES)

    sent = call(to_columns, shape(packet, bf16), (cm, orb, zf), late=(0, 1, 2), mib=ALL_MIB)
    planes = lax.all_to_all(sent, "pw", split_axis=0, concat_axis=0, tiled=True)
    index_scratch = [pltpu.VMEM(cm.shape, i32), pltpu.VMEM(cm.shape, i32)]
    pf_scratch = pltpu.VMEM((entries * nproj, BLOCK), f32)
    real_space, window, to_send, near = call(
        forward,
        (shape((blocks, 2 * BLOCK), bf16), shape((cj, SLOTS), f32), shape((count, cj, LANES), f32),
         shape((nproj * nproj, SLOTS), f32)),
        (cm, planes, yf, yft, xf, bi, at, proj, coup),
        index_scratch + [pltpu.VMEM((2 * z_local * PACK, 256), f32), pf_scratch],
        late=(0, 2, 3, 4, 8, 5, 7, 6),
    )
    other = lax.all_to_all(to_send, "pw", split_axis=0, concat_axis=0, tiled=True)
    all_planes = lax.all_gather(planes, "band", axis=0, tiled=False)
    all_orb = lax.all_gather(orb, "band", axis=0, tiled=False)
    back = call(
        backward, shape(packet, bf16),
        (cm, other, window, real_space, potential, near, bi, at, proj, xb, yb, ybt, all_planes, all_orb),
        index_scratch
        + [pf_scratch, pltpu.VMEM((2 * z_local * PACK, 256), bf16), pltpu.VMEM(packet, f32)]
        + [pltpu.VMEM((z_local * grid_x, LANES), f32)] * 2,
        late=(7, 8, 6, 4, 9, 10, 11, 0, 12, 13), mib=50,
    )
    returned = lax.all_to_all(back, "pw", split_axis=0, concat_axis=0, tiled=True)
    applied, sums = call(
        finish, (shape((2 * grid_z, col_local), f32), shape((2, 1, bands), f32)),
        (cm, orb, returned, zb),
    )
    applied = applied.reshape(1, 2, grid_z, col_local)
    return applied, sums.transpose(0, 2, 1)


def solution(mesh):
    in_specs = (
        P("band", None, None, "pw"),
        P(),
        P("pw", None, None),
        P("pw", None, None),
        P("pw"),
        P("pw"),
        P(),
    )
    out_specs = (P("band", None, None, "pw"), P(None, None, "band"))
    return jax.shard_map(
        per_device, mesh=mesh, in_specs=in_specs, out_specs=out_specs, check_vma=False
    )
```

```python
import math

import jax
import jax.numpy as jnp
import numpy as np
from jax import lax
from jax.experimental import pallas as pl
from jax.experimental.pallas import tpu as pltpu
from jax.sharding import PartitionSpec as P

KMAX = 73
BLOCK = 128
LANES = 128
VMEM_MIB, ALL_MIB = 52, 58
MAIN, TAIL = 80, 16
PACK = MAIN + TAIL
SLOTS = 256
kinetic_unit = 0.5 * (2.0 * math.pi / 58.6) ** 2
f32, bf16, i32 = jnp.float32, jnp.bfloat16, jnp.int32


def dft_table(length, sign):
    steps = np.arange(length, dtype=np.int32)
    product = steps[:, None] * steps[None, :] % length
    angles = product.astype(np.float32) * np.float32(2.0 * math.pi / length)
    root = np.float32(math.sqrt(length))
    cosines = np.cos(angles) / root
    sines = np.float32(sign) * np.sin(angles) / root
    return np.stack([np.stack([cosines, sines], 1), np.stack([-sines, cosines], 1)], 0).astype(np.float32)


def box_half(grid_x, grid_y, ncolumns):
    freq_x = np.arange(grid_x) - grid_x * (np.arange(grid_x) >= grid_x // 2)
    freq_y = np.arange(grid_y) - grid_y * (np.arange(grid_y) >= grid_y // 2)
    radius_sq = np.sort((freq_x[:, None] ** 2 + freq_y[None, :] ** 2).ravel())
    return int(math.isqrt(int(radius_sq[ncolumns - 1])))


def make_tables(grid_z, grid_x, grid_y, z_local, half):
    count = grid_z // z_local
    width = 2 * half + 1
    fwd_z, back_z = dft_table(grid_z, 1.0), dft_table(grid_z, -1.0)
    fwd_x, back_x = dft_table(grid_x, 1.0), dft_table(grid_x, -1.0)
    fwd_y, back_y = dft_table(grid_y, 1.0), dft_table(grid_y, -1.0)
    box_x = (np.arange(width) - half) % grid_x
    box_y = (np.arange(width) - half) % grid_y
    zf = np.zeros((count, 8, 2 * grid_z), np.float32)
    zb = np.zeros((2 * grid_z, count, 8), np.float32)
    for d in range(2):
        for plane in range(z_local):
            w = np.arange(count) * z_local + plane
            zf[:, d * z_local + plane, :] = fwd_z[:, :, d, w].reshape(2 * grid_z, count).T
            zb[:, :, d * z_local + plane] = back_z[d, w].reshape(count, 2 * grid_z).T
    split = LANES
    more = width - split
    pair = [np.arange(par, width, 2) for par in range(2)]
    beyond = [np.arange(split + par, width, 2) for par in range(2)]
    yf = np.zeros((2, split, 2, 256), np.float32)
    yf[:, :, :, :grid_y] = fwd_y[:, box_y[:split]]
    yft = np.zeros((2, 2, TAIL, 2, 256), np.float32)
    xf = np.zeros((2 * grid_x, 2, 2, MAIN), np.float32)
    xb = np.zeros((2, 2, MAIN, 2, grid_x), np.float32)
    order = np.concatenate([np.arange(0, grid_x, 2), np.arange(1, grid_x, 2)])
    yb = np.zeros((2, 256, 2, split), np.float32)
    yb[:, :grid_y] = back_y[:, :, :, box_y[:split]]
    ybt = np.zeros((2, 2, 2, TAIL, 256), np.float32)
    for par in range(2):
        xs, ys = box_x[pair[par]], box_y[beyond[par]]
        yft[:, par, : len(ys), :, :grid_y] = fwd_y[:, ys]
        for c in range(2):
            xf[:, c, par, : len(xs)] = fwd_x[c, xs][:, :, order].reshape(len(xs), 2 * grid_x).T
            for d in range(2):
                xb[d, par, : len(xs), c] = back_x[c, order][:, d, xs].T
                ybt[c, d, par, : len(ys), :grid_y] = back_y[c, :, d, ys]
    arrays = (
        zf.reshape(count * 8, -1), zb.reshape(2 * grid_z, -1), yf.reshape(2 * split, 512),
        yft.reshape(4 * TAIL, 512), xf.reshape(2 * grid_x, 4 * MAIN), xb.reshape(4 * MAIN, 2 * grid_x),
        yb.reshape(2, 256, 2 * split), ybt.reshape(2, 4 * TAIL, 256),
    )
    reach_x = math.isqrt((half + 1) ** 2 - 1 - (split - half) ** 2)
    assert (half + reach_x) // 2 < 64 and (more + 1) // 2 <= TAIL and half + 1 <= MAIN
    return [jnp.asarray(a.astype(jnp.bfloat16)) for a in arrays]


def dot(a, b, dims=((1,), (0,))):
    return lax.dot_general(a, b, (dims, ((), ())), preferred_element_type=f32)


def split3(x):
    hi = x.astype(bf16)
    rest = x - hi.astype(f32)
    mid = rest.astype(bf16)
    low = (rest - mid.astype(f32)).astype(bf16)
    return hi, mid, low


def iota(shape, axis):
    return lax.broadcasted_iota(i32, shape, axis)


def ones_where(mask):
    return jnp.where(mask, 1.0, 0.0).astype(bf16)


def quotient(values, divisor):
    return jnp.floor((values.astype(f32) + 0.5) * (1.0 / divisor)).astype(i32)


def frequencies(columns, grid_x, grid_y):
    x = quotient(columns, grid_y)
    y = columns - x * grid_y
    return jnp.where(x >= grid_x // 2, x - grid_x, x), jnp.where(y >= grid_y // 2, y - grid_y, y)


def radius_rows(p, cm_ref, grid_x, grid_y, grid_z):
    own = cm_ref[pl.ds(2 * p, 2), :]
    freq_x, freq_y = frequencies(own, grid_x, grid_y)
    flat = freq_x * freq_x + freq_y * freq_y
    row = iota((2 * grid_z, LANES), 0)
    z = jnp.where(row >= grid_z, row - grid_z, row)
    freq_z = jnp.where(z >= grid_z // 2, z - grid_z, z)
    sq = freq_z * freq_z
    return [sq + flat[h : h + 1, :] for h in range(2)]


def build(sizes):
    (grid_z, grid_x, grid_y, z_local, count, bands, natoms, nproj, entries, half) = sizes
    pairs = grid_x // 2
    blocks = z_local * grid_x * grid_y // BLOCK
    plane_blocks = blocks // z_local
    reach = natoms // count
    chunks = entries // LANES
    cj = 2 * nproj
    nch = 2 * z_local
    steps = 32
    gsteps = 32
    rows_c = z_local * PACK

    def block_rows(values):
        plane = quotient(values, plane_blocks)
        rest = values - plane * plane_blocks
        k = quotient(rest, 3)
        return plane * plane_blocks + (rest - 3 * k) * pairs + k

    def slots_of(values, p):
        start = p * natoms // count - 2 * reach
        t = values - start
        t = jnp.where(t < 0, t + natoms, t)
        return jnp.where(t >= natoms, t - natoms, t)

    def columns_of(rows):
        padded = jnp.concatenate([rows.astype(f32), jnp.zeros((8 - chunks, LANES), f32)], 0)
        return padded.T.astype(i32)

    def slot_onehot(at_ref, p):
        cols = columns_of(slots_of(at_ref[...], p))
        lane = iota((LANES, SLOTS), 1)
        return jnp.concatenate([ones_where(lane == cols[:, i : i + 1]) for i in range(chunks)], 0)

    def box_indices(cm_ref, row_ref, lane_ref):
        freq_x, freq_y = frequencies(cm_ref[...], grid_x, grid_y)
        x, y = freq_x + half, freq_y + half
        pair, parity, more = x >> 1, x & 1, y - LANES
        row_ref[...] = jnp.where(more >= 0, MAIN + (more >> 1), pair)
        lane_ref[...] = jnp.where(
            more >= 0, (more & 1) * LANES + parity * 64 + pair, parity * LANES + y
        )

    def near_coupling(p, coup):
        start = p * natoms // count - 2 * reach
        atom = start + iota((natoms, SLOTS), 1)
        atom = jnp.where(atom < 0, atom + natoms, atom)
        atom = jnp.where(atom >= natoms, atom - natoms, atom)
        select = ones_where(atom == iota((natoms, SLOTS), 0))
        near = dot(jnp.concatenate(split3(coup()[...]), 0), select)
        square = nproj * nproj
        return near[0:square] + near[square : 2 * square] + near[2 * square : 3 * square]

    def hot_rows(numbers, row, count):
        wide = jnp.broadcast_to(row.astype(f32), (16, LANES)).astype(bf16)
        same = numbers.reshape(count // 16, 16, LANES) == wide[None]
        return jnp.where(same, jnp.ones((), bf16), jnp.zeros((), bf16))

    def to_columns(cm, orb, table, out_ref):
        p = lax.axis_index("pw")
        radius = radius_rows(p, cm(), grid_x, grid_y, grid_z)
        orb_ref = orb()
        parts = []
        for h in range(2):
            values = orb_ref[:, h * LANES : (h + 1) * LANES].astype(f32)
            parts.append(jnp.where(radius[h] <= KMAX * KMAX, values, 0.0).astype(bf16))
        z = dot(table()[...], jnp.concatenate(parts, 1))
        out = [z[:, h * LANES : (h + 1) * LANES].reshape(count, 8, LANES) for h in range(2)]
        out_ref[...] = jnp.concatenate(out, 1).astype(bf16)

    def forward(cm, zr_ref, yf, yft, xf, bi, at, proj, coup,
                rs_ref, win_ref, send_ref, near_ref, xi_ref, yi_ref, acc_ref, pf_ref):
        p = lax.axis_index("pw")
        box_indices(cm(), xi_ref, yi_ref)
        acc_ref[...] = jnp.zeros_like(acc_ref)
        pack_row = iota((PACK, LANES), 0).astype(f32).astype(bf16)
        pack_lane = iota((256, LANES), 0).astype(f32).astype(bf16)

        def add_columns(step, carry):
            xrows = xi_ref[pl.ds(pl.multiple_of(step * 2 * steps, 8), 2 * steps), :]
            yrows = yi_ref[pl.ds(pl.multiple_of(step * 2 * steps, 8), 2 * steps), :]
            left, right = [], []
            for s in range(steps):
                v = zr_ref[step * steps + s].astype(f32)
                for h in range(2):
                    r = 2 * s + h
                    hot = hot_rows(pack_row, xrows[r : r + 1, :], PACK)
                    right.append(hot_rows(pack_lane, yrows[r : r + 1, :], 256).reshape(256, LANES))
                    rows = []
                    for ch in range(nch):
                        one = v[h * 8 + ch : h * 8 + ch + 1, :]
                        wide = jnp.broadcast_to(one, (16, LANES)).astype(bf16)
                        rows.append((hot * wide[None]).reshape(PACK, LANES))
                    left.append(jnp.concatenate(rows, 0))
            acc_ref[...] += dot(jnp.concatenate(left, 1), jnp.concatenate(right, 1), ((1,), (1,)))
            return carry

        lax.fori_loop(0, count // steps, add_columns, 0)
        yf_ref, yft_ref, xf_ref = yf(), yft(), xf()
        main, tails = [], []
        for plane in range(z_local):
            starts = [c * rows_c + plane * PACK for c in range(2)]
            for par in range(2):
                lanes = slice(par * LANES, (par + 1) * LANES)
                main.append(jnp.concatenate([acc_ref[r : r + MAIN, lanes] for r in starts], 1))
            tails.append(
                jnp.concatenate(
                    [
                        acc_ref[r + MAIN : r + PACK, par * LANES : (par + 1) * LANES]
                        for r in starts
                        for par in range(2)
                    ],
                    0,
                ).astype(bf16)
            )
        ydone = dot(jnp.concatenate(main, 0).astype(bf16), yf_ref[...])
        lane = iota((pairs, LANES), 1)
        for plane in range(z_local):
            more = dot(tails[plane], yft_ref[...], ((0,), (0,)))
            mine = []
            for par in range(2):
                r = (plane * 2 + par) * MAIN
                mine.append(ydone[r : r + 64] + more[par * 64 : (par + 1) * 64])
                mine.append(ydone[r + 64 : r + MAIN])
            mine = jnp.concatenate(mine, 0).astype(bf16)
            real = dot(xf_ref[...], jnp.concatenate([mine[:, 0:256], mine[:, 256:512]], 0))
            for d in range(2):
                even = real[d * grid_x : d * grid_x + pairs]
                odd = real[d * grid_x + pairs : (d + 1) * grid_x]
                turned = pltpu.roll(odd[:, 0:128], 64, 1)
                middle = jnp.where(lane < 64, even[:, 128:256], turned)
                last = jnp.where(lane < 64, turned, pltpu.roll(odd[:, 128:256], 64, 1))
                for t, piece in enumerate((even[:, 0:128], middle, last)):
                    own = plane * plane_blocks + t * pairs
                    rs_ref[own : own + pairs, d * BLOCK : (d + 1) * BLOCK] = piece.astype(bf16)
        near_ref[...] = near_coupling(p, coup)
        pf_ref[...] = proj()[...].astype(f32)
        cols = columns_of(block_rows(bi()[...]))
        block_lane = iota((LANES, blocks), 1)
        hot = jnp.concatenate(
            [ones_where(block_lane == cols[:, i : i + 1]) for i in range(chunks)], 0
        )
        picked = dot(hot, rs_ref[...])
        select_row = iota((2 * BLOCK, LANES), 0)
        select_lane = iota((2 * BLOCK, LANES), 1)
        products, selects = [], []
        for j in range(nproj):
            values = pf_ref[pl.ds(j, entries, stride=nproj), :]
            product = jnp.concatenate([values, values], 1) * picked
            hi = product.astype(bf16)
            products += [hi, (product - hi.astype(f32)).astype(bf16)]
            selects += [ones_where(select_lane == jnp.where(select_row >= BLOCK, nproj + j, j))] * 2
        corr = dot(jnp.concatenate(products, 1), jnp.concatenate(selects, 0))
        pieces = jnp.concatenate(split3(corr), 1)
        window = dot(pieces, slot_onehot(at(), p), ((0,), (0,)))
        window = window[0:cj] + window[LANES : LANES + cj] + window[2 * LANES : 2 * LANES + cj]
        win_ref[...] = window
        send_ref[...] = jnp.zeros_like(send_ref)
        home = p * natoms // count
        for s in range(1, 5):
            up = lax.rem(p + s, count)
            ahead = up * natoms // count - home
            ahead = jnp.where(ahead < 0, ahead + natoms, ahead)
            send_ref[up] = pltpu.roll(window, SLOTS - ahead, 1)[:, 0:LANES]
            down = lax.rem(p - s + count, count)
            send_ref[down] = window[:, 0:LANES]

    def backward(cm, xr_ref, win_ref, rs_ref, potential, near_ref, bi, at, proj,
                 xb, yb, ybt, zall, oall, out_ref,
                 xi_ref, yi_ref, pf_ref, grid_ref, ret_ref, pot_first, pot_rest):
        p = lax.axis_index("pw")
        home = p * natoms // count
        total = win_ref[...]
        nothing = jnp.zeros((cj, LANES), f32)
        for s in range(1, 5):
            down = lax.rem(p - s + count, count)
            total = total + jnp.concatenate([xr_ref[down], nothing], 1)
            up = lax.rem(p + s, count)
            ahead = up * natoms // count - home
            ahead = jnp.where(ahead < 0, ahead + natoms, ahead)
            total = total + pltpu.roll(jnp.concatenate([xr_ref[up], nothing], 1), ahead, 1)
        near = near_ref[...]
        near = near.reshape(nproj, nproj, SLOTS)
        weight = jnp.concatenate(
            [jnp.sum(near * total[c * nproj : (c + 1) * nproj][None], 1) for c in range(2)], 0
        ).astype(bf16)
        pf_ref[...] = proj()[...].astype(f32)
        ent_weight = dot(slot_onehot(at(), p), weight, ((1,), (1,)))
        ent_weight = ent_weight.astype(bf16)
        spread_row = iota((cj, 2 * BLOCK), 0)
        spread_part = jnp.where(iota((cj, 2 * BLOCK), 1) >= BLOCK, nproj, 0)
        terms = jnp.zeros((entries, 2 * BLOCK), f32)
        for j in range(nproj):
            values = pf_ref[pl.ds(j, entries, stride=nproj), :]
            wide = dot(ent_weight, ones_where(spread_row == spread_part + j))
            terms = terms + wide * jnp.concatenate([values, values], 1)
        pieces = jnp.concatenate(split3(terms), 1)
        rows = block_rows(bi()[...])
        block_row = iota((blocks, LANES), 0)
        hot = jnp.concatenate(
            [ones_where(block_row == rows[i : i + 1, :]) for i in range(chunks)], 1
        )
        nonlocal_part = dot(hot, pieces)
        nonlocal_part = (
            nonlocal_part[:, 0:256] + nonlocal_part[:, 256:512] + nonlocal_part[:, 512:768]
        )
        pot_ref = potential()
        pot_first[...] = pot_ref[:, :, 0:LANES].reshape(z_local * grid_x, LANES)
        pot_rest[:, 0 : grid_y - LANES] = pot_ref[:, :, LANES:grid_y].reshape(
            z_local * grid_x, grid_y - LANES
        )
        xb_ref, yb_ref, ybt_ref = xb(), yb(), ybt()
        lane = iota((pairs, LANES), 1)
        backs = [[], []]
        for plane in range(z_local):
            first = plane * plane_blocks
            even, odd = (
                [
                    part[pl.ds(plane * grid_x + parity, pairs, stride=2), :]
                    for part in (pot_first, pot_rest)
                ]
                for parity in range(2)
            )
            turned = pltpu.roll(odd[0], 64, 1)
            pot = (
                even[0],
                jnp.where(lane < 64, even[1], turned),
                jnp.where(lane < 64, turned, pltpu.roll(odd[1], 64, 1)),
            )
            stacked = []
            for c in range(2):
                h = []
                for t in range(3):
                    own = slice(first + t * pairs, first + (t + 1) * pairs)
                    lanes = slice(c * BLOCK, (c + 1) * BLOCK)
                    h.append(pot[t] * rs_ref[own, lanes].astype(f32) + nonlocal_part[own, lanes])
                swung = pltpu.roll(h[2], 64, 1)
                stacked.append(jnp.concatenate([h[0], jnp.where(lane < 64, h[1], 0.0)], 1))
                stacked.append(
                    jnp.concatenate(
                        [
                            jnp.where(lane < 64, pltpu.roll(h[1], 64, 1), swung),
                            jnp.where(lane < 64, swung, 0.0),
                        ],
                        1,
                    )
                )
            x_back = dot(xb_ref[...], jnp.concatenate(stacked, 0).astype(bf16)).astype(bf16)
            tail = jnp.zeros((4 * TAIL, LANES), f32)
            for c in range(2):
                mine = x_back[c * 2 * MAIN : (c + 1) * 2 * MAIN]
                backs[c].append(mine)
                near_rows = jnp.concatenate([mine[0:64], mine[MAIN : MAIN + 64]], 0)
                tail = tail + dot(ybt_ref[c], near_rows, ((1,), (1,)))
            for d in range(2):
                for par in range(2):
                    r = d * rows_c + plane * PACK + MAIN
                    own = (2 * d + par) * TAIL
                    grid_ref[r : r + TAIL, par * LANES : (par + 1) * LANES] = tail[
                        own : own + TAIL
                    ].astype(bf16)
        y_back = dot(jnp.concatenate(backs[0], 0), yb_ref[0]) + dot(
            jnp.concatenate(backs[1], 0), yb_ref[1]
        )
        for plane in range(z_local):
            for par in range(2):
                own = (plane * 2 + par) * MAIN
                for d in range(2):
                    r = d * rows_c + plane * PACK
                    grid_ref[r : r + MAIN, par * LANES : (par + 1) * LANES] = y_back[
                        own : own + MAIN, d * LANES : (d + 1) * LANES
                    ].astype(bf16)
        cm_ref, zall_ref = cm(), zall()
        box_indices(cm_ref, xi_ref, yi_ref)
        pack_row = iota((PACK, LANES), 0).astype(f32).astype(bf16)
        pack_lane = iota((256, LANES), 0).astype(f32).astype(bf16)
        blank = jnp.zeros((8 - nch, LANES), f32)

        def take_columns(step, carry):
            base = pl.multiple_of(step * 2 * gsteps, 8)
            xrows = xi_ref[pl.ds(base, 2 * gsteps), :]
            yrows = yi_ref[pl.ds(base, 2 * gsteps), :]
            sums = list(carry)
            for s in range(gsteps):
                hot_y = jnp.concatenate(
                    [hot_rows(pack_lane, yrows[2 * s + h : 2 * s + h + 1, :], 256).reshape(256, LANES) for h in range(2)], 1
                )
                taken = dot(grid_ref[...], hot_y)
                halves, swapped = [], []
                for h in range(2):
                    mask = hot_rows(pack_row, xrows[2 * s + h : 2 * s + h + 1, :], PACK).reshape(PACK, LANES)
                    rows = []
                    for ch in range(nch):
                        part = taken[ch * PACK : (ch + 1) * PACK, h * LANES : (h + 1) * LANES]
                        part = (part.astype(bf16) * mask).reshape(PACK // 16, 16, LANES)
                        own = part[0]
                        for k in range(1, PACK // 16):
                            own = own + part[k]
                        rows.append(jnp.sum(own.astype(f32), 0, keepdims=True))
                    halves.append(jnp.concatenate(rows + [blank], 0))
                    other = rows[z_local:] + [-r for r in rows[:z_local]]
                    swapped.append(jnp.concatenate(other + [blank], 0))
                ret = jnp.concatenate(halves, 0)
                cross = jnp.concatenate(swapped, 0)
                ret_ref[step * gsteps + s] = ret
                for m in range(bands):
                    other = zall_ref[m, step * gsteps + s].astype(f32)
                    sums[m] = sums[m] + other * ret
                    sums[bands + m] = sums[bands + m] + other * cross
            return tuple(sums)

        zero = jnp.zeros((16, LANES), f32)
        sums = lax.fori_loop(0, count // gsteps, take_columns, (zero,) * (2 * bands))
        radius = radius_rows(p, cm_ref, grid_x, grid_y, grid_z)
        band = lax.axis_index("band")
        oall_ref = oall()
        kin = [jnp.zeros((1, LANES), f32) for _ in range(2 * bands)]
        for h in range(2):
            lanes = slice(h * LANES, (h + 1) * LANES)
            own = oall_ref[band, :, lanes].astype(f32)
            kinetic = jnp.where(radius[h] <= KMAX * KMAX, kinetic_unit * radius[h].astype(f32), 0.0)
            own = kinetic * own
            for m in range(bands):
                other = oall_ref[m, :, lanes].astype(f32)
                kin[m] = kin[m] + jnp.sum(other * own, 0, keepdims=True)
                kin[bands + m] = kin[bands + m] + jnp.sum(
                    other[:grid_z] * own[grid_z:] - other[grid_z:] * own[:grid_z], 0, keepdims=True
                )
        lane = iota((1, LANES), 1)
        row = jnp.zeros((1, LANES), f32)
        for n in range(2 * bands):
            value = jnp.sum(sums[n], 0, keepdims=True) + kin[n]
            value = jnp.sum(value, 1, keepdims=True)
            for k, piece in enumerate(split3(value)):
                row = jnp.where(lane == 2 * bands * k + n, piece.astype(f32), row)
        sub = iota((16, LANES), 0)
        carried = jnp.where(sub == nch, jnp.broadcast_to(row, (16, LANES)), 0.0)
        out_ref[...] = (ret_ref[...] + carried[None]).astype(bf16)

    def finish(cm_ref, orb_ref, rr_ref, tab_ref, applied_ref, sub_ref):
        p = lax.axis_index("pw")
        radius = radius_rows(p, cm_ref, grid_x, grid_y, grid_z)
        got = rr_ref[...].astype(f32)
        right = jnp.concatenate(
            [got[:, h * 8 : (h + 1) * 8].reshape(count * 8, LANES) for h in range(2)], 1
        ).astype(bf16)
        z_back = dot(tab_ref[...], right)
        for h in range(2):
            lanes = slice(h * LANES, (h + 1) * LANES)
            values = orb_ref[:, lanes].astype(f32)
            result = kinetic_unit * radius[h].astype(f32) * values + z_back[:, lanes]
            applied_ref[:, lanes] = jnp.where(radius[h] <= KMAX * KMAX, result, 0.0)
        summed = jnp.sum(got[:, 0:8], 0)
        summed = summed + (
            pltpu.roll(summed, LANES - 2 * bands, 1) + pltpu.roll(summed, LANES - 4 * bands, 1)
        )
        summed = summed[nch : nch + 1] * (1.0 / (grid_z * count * 2 * LANES))
        sub_ref[0] = summed[:, 0:bands]
        sub_ref[1] = pltpu.roll(summed, LANES - bands, 1)[:, 0:bands]

    return to_columns, forward, backward, finish


class Late:
    def __init__(self, source, target, semaphore):
        self.copy = pltpu.make_async_copy(source, target, semaphore)
        self.target = target
        self.waiting = True
        self.copy.start()

    def __call__(self):
        if self.waiting:
            self.copy.wait()
            self.waiting = False
        return self.target


def call(kernel, out_shape, operands, scratch=(), late=(), mib=VMEM_MIB):
    vmem = pl.BlockSpec(memory_space=pltpu.VMEM)
    hbm = pl.BlockSpec(memory_space=pltpu.HBM)
    multiple = isinstance(out_shape, (list, tuple))
    n_in, n_out, n_own = len(operands), len(out_shape) if multiple else 1, len(scratch)

    def body(*refs):
        given, rest = list(refs[:n_in]), refs[n_in : n_in + n_out + n_own]
        if late:
            buffers, semaphores = refs[n_in + n_out + n_own : -1], refs[-1]
            for k, at in enumerate(late):
                given[at] = Late(given[at], buffers[k], semaphores.at[k])
        kernel(*given, *rest)

    extra = [pltpu.VMEM(operands[at].shape, operands[at].dtype) for at in late]
    if late:
        extra.append(pltpu.SemaphoreType.DMA((len(late),)))
    return pl.pallas_call(
        body,
        out_shape=out_shape,
        in_specs=[hbm if at in late else vmem for at in range(n_in)],
        out_specs=[vmem] * n_out if multiple else vmem,
        scratch_shapes=list(scratch) + extra,
        compiler_params=pltpu.CompilerParams(vmem_limit_bytes=mib * 1024 * 1024),
    )(*operands)


def per_device(orbitals, column_map, potential, projectors, block_index, block_atom, coupling):
    _, _, grid_z, col_local = orbitals.shape
    z_local, grid_x, grid_y = potential.shape
    natoms, nproj = coupling.shape[0], coupling.shape[1]
    entries = block_index.shape[0]
    count, bands = lax.axis_size("pw"), lax.axis_size("band")
    ncolumns = column_map.shape[0]
    half = box_half(grid_x, grid_y, ncolumns)
    zf, zb, yf, yft, xf, xb, yb, ybt = make_tables(grid_z, grid_x, grid_y, z_local, half)
    sizes = (grid_z, grid_x, grid_y, z_local, count, bands, natoms, nproj, entries, half)
    to_columns, forward, backward, finish = build(sizes)
    shape = jax.ShapeDtypeStruct
    blocks = z_local * grid_x * grid_y // BLOCK
    cj = 2 * nproj

    cm = column_map.reshape(ncolumns // LANES, LANES)
    orb = orbitals.reshape(2 * grid_z, col_local)
    bi = block_index.reshape(entries // LANES, LANES)
    at = block_atom.reshape(entries // LANES, LANES)
    coup = coupling.reshape(natoms, nproj * nproj).T
    proj = projectors.reshape(entries * nproj, BLOCK)
    packet = (count, 16, LANES)

    sent = call(to_columns, shape(packet, bf16), (cm, orb, zf), late=(0, 1, 2), mib=ALL_MIB)
    planes = lax.all_to_all(sent, "pw", split_axis=0, concat_axis=0, tiled=True)
    index_scratch = [pltpu.VMEM(cm.shape, i32), pltpu.VMEM(cm.shape, i32)]
    pf_scratch = pltpu.VMEM((entries * nproj, BLOCK), f32)
    real_space, window, to_send, near = call(
        forward,
        (shape((blocks, 2 * BLOCK), bf16), shape((cj, SLOTS), f32), shape((count, cj, LANES), f32),
         shape((nproj * nproj, SLOTS), f32)),
        (cm, planes, yf, yft, xf, bi, at, proj, coup),
        index_scratch + [pltpu.VMEM((2 * z_local * PACK, 256), f32), pf_scratch],
        late=(0, 2, 3, 4, 8, 5, 7, 6),
    )
    other = lax.all_to_all(to_send, "pw", split_axis=0, concat_axis=0, tiled=True)
    all_planes = lax.all_gather(planes, "band", axis=0, tiled=False)
    all_orb = lax.all_gather(orb, "band", axis=0, tiled=False)
    back = call(
        backward, shape(packet, bf16),
        (cm, other, window, real_space, potential, near, bi, at, proj, xb, yb, ybt, all_planes, all_orb),
        index_scratch
        + [pf_scratch, pltpu.VMEM((2 * z_local * PACK, 256), bf16), pltpu.VMEM(packet, f32)]
        + [pltpu.VMEM((z_local * grid_x, LANES), f32)] * 2,
        late=(7, 8, 6, 4, 9, 10, 11, 0, 12, 13), mib=50,
    )
    returned = lax.all_to_all(back, "pw", split_axis=0, concat_axis=0, tiled=True)
    applied, sums = call(
        finish, (shape((2 * grid_z, col_local), f32), shape((2, 1, bands), f32)),
        (cm, orb, returned, zb),
    )
    applied = applied.reshape(1, 2, grid_z, col_local)
    return applied, sums.transpose(0, 2, 1)


def solution(mesh):
    in_specs = (
        P("band", None, None, "pw"),
        P(),
        P("pw", None, None),
        P("pw", None, None),
        P("pw"),
        P("pw"),
        P(),
    )
    out_specs = (P("band", None, None, "pw"), P(None, None, "band"))
    return jax.shard_map(
        per_device, mesh=mesh, in_specs=in_specs, out_specs=out_specs, check_vma=False
    )
```
